32 devices in a mesh: ctx: 16 (over z, x, core), tp: 2 (over y).
Axes of the slice: x: 2, y: 2, z: 4, core: 2. Of those that a mesh axis runs over, the one named last changes fastest.
Arguments:
- hyena_q: bfloat16 [2048, 8192], P('ctx', 'tp'), may hold values from -36 to 36
- hyena_k: bfloat16 [2048, 8192], P('ctx', 'tp'), may hold values from -6 to 6
- hyena_v: bfloat16 [2048, 8192], P('ctx', 'tp'), may hold values from -6 to 6
- filter_rate: float32 [8192, 16], P('tp'), may hold values from 0 to 1, as said below
- filter_residue: float32 [8192, 16], P('tp'), may hold values from -0.12 to 0.12
- skip_gain: float32 [8192], P('tp'), may hold values from 0.5 to 1.5
Outputs:
- hyena_out: bfloat16 [2048, 8192], P('ctx', 'tp')
The draws below stay inside these ranges and needn't reach their ends.
Inputs may be any that keep to these rules, and one draw needn't show every extreme that they name: `filter_rate`: every rate is positive and at most 0.05.
All inputs are finite; a program needn't handle non-finite values.
Results may differ from the reference program's by a relative error of at most 0.0057.
Values may be sent and summed in bfloat16 or wider, within the bound.
A program may use at most 64 MiB of HBM per device.

```python
import jax
import jax.numpy as jnp
from jax import lax

D = 8192
ORDER = 16
SEQ = 2048


def draw_hyena_q(key, part):
    base = jax.random.fold_in(key, 77)
    key_a = jax.random.fold_in(base, 0)
    key_c = jax.random.fold_in(base, 2)
    columns = jnp.arange(D, dtype=jnp.float32) / (D - 1)
    chan_scale = 0.3 * jnp.exp(columns * jnp.log(10.0))
    row_scale = 0.3 * jnp.exp(jax.random.uniform(key_a, (SEQ,), jnp.float32) * jnp.log(10.0))
    values = jnp.clip(jax.random.normal(key_c, (SEQ, D), jnp.float32), -4.0, 4.0)
    return (values * row_scale[:, None] * chan_scale[None, :]).astype(jnp.bfloat16)


def draw_filter_rate(key, part):
    base = jax.random.fold_in(key, 31)
    key_a = jax.random.fold_in(base, 0)
    slowest = jnp.log(0.5 / SEQ)
    fastest = jnp.log(0.05)
    level = jax.random.uniform(key_a, (D, ORDER), jnp.float32)
    return jnp.exp(slowest + level * (fastest - slowest))


def levels(own_key, dims, pieces, smallest, top_value):
    def one(dim, blocks):
        draws = jax.random.uniform(jax.random.fold_in(jax.random.fold_in(own_key, 6), dim), (blocks,), jnp.float32, smallest / len(pieces), top_value / len(pieces))
        return jnp.repeat(jnp.exp(draws), dims[dim] // blocks).reshape((-1,) + (1,) * (len(dims) - dim - 1))

    gain = one(*pieces[0])
    for cut in pieces[1:]:
        gain = gain * one(*cut)
    return gain


def noise(stream_key, shape, scale, limit, shards=(), kind=jnp.bfloat16):
    array = jax.random.normal(stream_key, shape, jnp.float32) * scale
    if len(shards) > 0:
        array = levels(stream_key, shape, shards, -0.22, 0.18) * array
    return jnp.clip(array, min=-limit, max=limit).astype(kind)


def setup_inputs(seed: int = 0) -> dict:
    seeds = jax.random.split(jax.random.key(seed), 7)
    return {
        "hyena_q": draw_hyena_q(jax.random.fold_in(seeds[6], 71), 0),
        "hyena_k": noise(seeds[1], (SEQ, D), 1.0, 6.0, ((0, 16), (1, 2))),
        "hyena_v": noise(seeds[2], (SEQ, D), 1.0, 6.0, ((0, 16), (1, 2))),
        "filter_rate": draw_filter_rate(jax.random.fold_in(seeds[6], 71), 0),
        "filter_residue": noise(seeds[4], (D, ORDER), 0.02, 0.12, ((0, 2),), jnp.float32),
        "skip_gain": jnp.clip(0.5 + 1.0 * jax.random.uniform(seeds[5], (D,), jnp.float32) ** levels(seeds[5], (D,), ((0, 2),), -0.2, 0.2), 0.5, 1.5),
    }


def reference(hyena_q, hyena_k, hyena_v, filter_rate, filter_residue, skip_gain):
    product = (hyena_k.astype(jnp.float32) * hyena_v.astype(jnp.float32)).astype(jnp.bfloat16)
    steps = jnp.arange(SEQ, dtype=jnp.float32)
    filters = jnp.zeros((D, SEQ), jnp.float32)
    for mode in range(ORDER):
        filters = filters + filter_residue[:, mode:mode + 1] * jnp.exp(-filter_rate[:, mode:mode + 1] * steps[None, :])
    length = 2 * SEQ
    spectrum = jnp.fft.rfft(product.astype(jnp.float32).T, n=length, axis=1) * jnp.fft.rfft(filters, n=length, axis=1)
    convolved = jnp.fft.irfft(spectrum, n=length, axis=1)[:, :SEQ].T
    gated = (hyena_q.astype(jnp.float32) * (convolved + skip_gain[None, :] * product.astype(jnp.float32))).astype(jnp.bfloat16)
    gated_wide = gated.astype(jnp.float32)
    sumsq = lax.optimization_barrier(jnp.sum(gated_wide * gated_wide, axis=1, keepdims=True))
    return (gated_wide / jnp.sqrt(sumsq / D + 1e-06)).astype(jnp.bfloat16)
```

```python
import functools
import math

import jax
import jax.numpy as jnp
from jax import lax
from jax.experimental import pallas as pl
from jax.experimental.pallas import tpu as pltpu
from jax.sharding import PartitionSpec as P

D = 8192
ORDER = 16
LANES = 128
SUB = 8
WIDE = SUB * LANES
STEP = 16
MESH = pl.DeviceIdType.MESH


def kernel(
    n,
    ntp,
    n_own,
    q_hbm,
    k_hbm,
    v_hbm,
    rate_ref,
    res_ref,
    skip_ref,
    gated_hbm,
    sums_ref,
    qv,
    kv,
    vv,
    gv,
    rate_s,
    res_s,
    decay_s,
    taps_s,
    pos,
    fir,
    held,
    ends,
    ends_in,
    carry_out,
    carry,
    squares,
    sums_own,
    sums_in,
    q_sem,
    k_sem,
    v_sem,
    g_sem,
    end_send,
    end_recv,
    carry_send,
    carry_recv,
    sum_send,
    sum_recv,
):
    rows, width = q_hbm.shape
    groups = width // WIDE
    blocks = rows // STEP
    tiles = width // LANES
    keep = ORDER * groups // n_own
    spread = n // n_own
    per_group = ORDER // keep
    me = lax.axis_index("ctx")
    me_tp = lax.axis_index("tp")
    own = me // spread

    def cols(g):
        return pl.ds(pl.multiple_of(g * WIDE, WIDE), WIDE)

    def load_copy(src, dst, sem, g):
        return pltpu.make_async_copy(src.at[:, cols(g)], dst.at[g], sem.at[g])

    def out_copy(g):
        return pltpu.make_async_copy(gv.at[g], gated_hbm.at[:, cols(g)], g_sem.at[g])

    def first_group(j):
        return lax.rem(own // per_group + 1 + j, groups)

    def last_group(j):
        return lax.rem(own // per_group + j, groups)

    def end_copy(owner):
        return pltpu.make_async_remote_copy(
            src_ref=ends.at[pl.ds(owner * keep, keep)],
            dst_ref=ends_in.at[me],
            send_sem=end_send.at[owner],
            recv_sem=end_recv.at[me],
            device_id={"ctx": owner * spread},
            device_id_type=MESH,
        )

    def end_arrival(sender):
        return pltpu.make_async_remote_copy(
            src_ref=ends.at[pl.ds(0, keep)],
            dst_ref=ends_in.at[sender],
            send_sem=end_send.at[0],
            recv_sem=end_recv.at[sender],
            device_id={"ctx": sender},
            device_id_type=MESH,
        )

    def carry_copy(target):
        return pltpu.make_async_remote_copy(
            src_ref=carry_out.at[target],
            dst_ref=carry.at[pl.ds(own * keep, keep)],
            send_sem=carry_send.at[target],
            recv_sem=carry_recv.at[own],
            device_id={"ctx": target},
            device_id_type=MESH,
        )

    def carry_arrival(owner):
        return pltpu.make_async_remote_copy(
            src_ref=carry_out.at[0],
            dst_ref=carry.at[pl.ds(owner * keep, keep)],
            send_sem=carry_send.at[0],
            recv_sem=carry_recv.at[owner],
            device_id={"ctx": owner * spread},
            device_id_type=MESH,
        )

    def sum_copy(target):
        return pltpu.make_async_remote_copy(
            src_ref=sums_own,
            dst_ref=sums_in.at[me_tp],
            send_sem=sum_send.at[target],
            recv_sem=sum_recv.at[me_tp],
            device_id={"tp": target},
            device_id_type=MESH,
        )

    def sum_arrival(sender):
        return pltpu.make_async_remote_copy(
            src_ref=sums_own,
            dst_ref=sums_in.at[sender],
            send_sem=sum_send.at[0],
            recv_sem=sum_recv.at[sender],
            device_id={"tp": sender},
            device_id_type=MESH,
        )

    def load_group(j, _):
        g = first_group(j)
        load_copy(k_hbm, kv, k_sem, g).start()
        load_copy(v_hbm, vv, v_sem, g).start()
        return 0

    lax.fori_loop(0, groups, load_group, 0)

    def load_gate(j, _):
        load_copy(q_hbm, qv, q_sem, last_group(j)).start()
        return 0

    lax.fori_loop(0, groups, load_gate, 0)

    barrier = pltpu.get_barrier_semaphore()

    def greet_ctx(d, _):
        @pl.when(d != me)
        def _():
            pl.semaphore_signal(
                barrier, inc=1, device_id={"ctx": d}, device_id_type=MESH
            )

        return 0

    def greet_tp(d, _):
        @pl.when(d != me_tp)
        def _():
            pl.semaphore_signal(
                barrier, inc=1, device_id={"tp": d}, device_id_type=MESH
            )

        return 0

    lax.fori_loop(0, n, greet_ctx, 0)
    lax.fori_loop(0, ntp, greet_tp, 0)

    for tile in range(tiles):
        lanes = slice(tile * LANES, (tile + 1) * LANES)
        rate_s[tile * ORDER : (tile + 1) * ORDER, :] = rate_ref[:, lanes]
        res_s[tile * ORDER : (tile + 1) * ORDER, :] = res_ref[:, lanes]

    def mode_row(ref, g, mode):
        return ref[pl.ds(g * (SUB * ORDER) + mode, SUB, stride=ORDER), :]

    def position(g, t):
        return pl.ds(g * (SUB * rows) + t, SUB, stride=rows)

    def tile_rows(g, tile):
        return pl.ds(pl.multiple_of((g * SUB + tile) * rows, rows), rows)

    def local_states(j, _):
        g = first_group(j)
        load_copy(k_hbm, kv, k_sem, g).wait()
        load_copy(v_hbm, vv, v_sem, g).wait()
        for tile in range(SUB):
            lanes = slice(tile * LANES, (tile + 1) * LANES)
            wide = kv[g, :, lanes].astype(jnp.float32) * vv[g, :, lanes].astype(
                jnp.float32
            )
            pos[tile_rows(g, tile), :] = wide.astype(jnp.bfloat16).astype(jnp.float32)
        decay = [jnp.exp(-mode_row(rate_s, g, mode)) for mode in range(ORDER)]
        for mode in range(ORDER):
            decay_s[g, mode] = decay[mode]

        def block(b, states):
            states = list(states)
            for mode in range(ORDER):
                held[g, b, mode] = states[mode]
            for i in range(STEP):
                here = pos[position(g, b * STEP + i), :]
                for mode in range(ORDER):
                    states[mode] = states[mode] * decay[mode] + here
            return tuple(states)

        zero = jnp.zeros((SUB, LANES), jnp.float32)
        states = lax.fori_loop(0, blocks, block, (zero,) * ORDER)
        for mode in range(ORDER):
            ends[g * ORDER + mode] = states[mode]

        @pl.when(j == 0)
        def _():
            pl.semaphore_wait(barrier, n - 1 + ntp - 1)

        for part in range(per_group):
            owner = g * per_group + part

            @pl.when(owner * spread != me)
            def _():
                end_copy(owner).start()

        return 0

    lax.fori_loop(0, groups, local_states, 0)

    def near(g, _):
        skip = skip_ref[pl.ds(pl.multiple_of(g * SUB, SUB), SUB), :]
        weights = [mode_row(res_s, g, mode) for mode in range(ORDER)]
        taps = []
        for i in range(STEP):
            tap = functools.reduce(lambda x, y: x + y, weights)
            taps.append(tap + skip if i == 0 else tap)
            if i < STEP - 1:
                weights = [weights[mode] * decay_s[g, mode] for mode in range(ORDER)]
        for i in range(STEP):
            taps_s[i] = taps[i]

        def block(b, _):
            here = [pos[position(g, b * STEP + i), :] for i in range(STEP)]
            for i in range(STEP):
                total = taps_s[0] * here[i]
                for back in range(1, i + 1):
                    total = total + taps_s[back] * here[i - back]
                fir[g, b * STEP + i] = total
            return 0

        lax.fori_loop(0, blocks, block, 0)
        return 0

    lax.fori_loop(0, groups, near, 0)

    def own_scan():
        far = []
        for r in range(keep):
            row = own * keep + r
            far.append(
                jnp.exp(-float(rows) * mode_row(rate_s, row // ORDER, row % ORDER))
            )
        ends_in[me] = ends[pl.ds(own * keep, keep)]

        def device(d, states):
            states = list(states)
            for r in range(keep):
                carry_out[d, r] = states[r]

            @pl.when(d != me)
            def _():
                carry_copy(d).start()
                end_arrival(d).wait_recv()

            for r in range(keep):
                states[r] = states[r] * far[r] + ends_in[d, r]
            return tuple(states)

        zero = jnp.zeros((SUB, LANES), jnp.float32)
        lax.fori_loop(0, n, device, (zero,) * keep)
        carry[pl.ds(own * keep, keep)] = carry_out[me]

    if spread == 1:
        own_scan()
    else:
        pl.when(lax.rem(me, spread) == 0)(own_scan)

    squares[...] = jnp.zeros_like(squares)

    def finish(j, _):
        g = last_group(j)
        for part in range(per_group):
            owner = g * per_group + part

            @pl.when(owner * spread != me)
            def _():
                carry_arrival(owner).wait_recv()

        def block(b, _):
            terms = []
            for mode in range(ORDER):
                state = carry[g * ORDER + mode]
                terms.append(
                    mode_row(res_s, g, mode) * (held[g, b, mode] + state)
                )
                step = decay_s[g, mode]
                for _ in range(int(math.log2(STEP))):
                    step = step * step
                carry[g * ORDER + mode] = state * step
            for i in range(STEP):
                terms = [terms[mode] * decay_s[g, mode] for mode in range(ORDER)]
                tree = [fir[g, b * STEP + i]] + terms
                while len(tree) > 1:
                    pairs = [
                        tree[x] + tree[x + 1] for x in range(0, len(tree) - 1, 2)
                    ]
                    tree = pairs + tree[len(tree) // 2 * 2 :]
                pos[position(g, b * STEP + i), :] = tree[0]
            return 0

        lax.fori_loop(0, blocks, block, 0)
        load_copy(q_hbm, qv, q_sem, g).wait()
        for tile in range(SUB):
            lanes = slice(tile * LANES, (tile + 1) * LANES)
            gated = (
                qv[g, :, lanes].astype(jnp.float32) * pos[tile_rows(g, tile), :]
            ).astype(jnp.bfloat16)
            gv[g, :, lanes] = gated
            wide = gated.astype(jnp.float32)
            squares[...] += wide * wide
        out_copy(g).start()
        return 0

    lax.fori_loop(0, groups, finish, 0)

    sums_own[...] = lax.dot_general(
        jnp.ones((SUB, LANES), jnp.float32),
        squares[...],
        (((1,), (1,)), ((), ())),
        precision=lax.Precision.HIGHEST,
        preferred_element_type=jnp.float32,
    )

    def send_sum(d, _):
        @pl.when(d != me_tp)
        def _():
            sum_copy(d).start()

        return 0

    lax.fori_loop(0, ntp, send_sum, 0)
    sums_in[me_tp] = sums_own[...]

    def drain_out(g, _):
        out_copy(g).wait()
        return 0

    lax.fori_loop(0, groups, drain_out, 0)

    def drain_ends(owner, _):
        @pl.when(owner * spread != me)
        def _():
            end_copy(owner).wait_send()

        return 0

    lax.fori_loop(0, n_own, drain_ends, 0)

    def drain_carry():
        def one(d, _):
            @pl.when(d != me)
            def _():
                carry_copy(d).wait_send()

            return 0

        lax.fori_loop(0, n, one, 0)

    if spread == 1:
        drain_carry()
    else:
        pl.when(lax.rem(me, spread) == 0)(drain_carry)

    def take_sum(d, _):
        @pl.when(d != me_tp)
        def _():
            sum_arrival(d).wait_recv()
            sum_copy(d).wait_send()

        return 0

    lax.fori_loop(0, ntp, take_sum, 0)
    total = sums_in[0]
    for d in range(1, ntp):
        total = total + sums_in[d]
    sums_ref[...] = total


def per_device(n, ntp, hyena_q, hyena_k, hyena_v, filter_rate, filter_residue, skip):
    rows, width = hyena_q.shape
    groups = width // WIDE
    n_own = min(n, ORDER * groups)
    keep = ORDER * groups // n_own
    tiles = width // LANES
    f32, bf16 = jnp.float32, jnp.bfloat16
    any_space = pl.BlockSpec(memory_space=pl.ANY)
    vmem = pl.BlockSpec(memory_space=pltpu.VMEM)
    dma = pltpu.SemaphoreType.DMA
    gated, sums = pl.pallas_call(
        functools.partial(kernel, n, ntp, n_own),
        out_shape=(
            jax.ShapeDtypeStruct((rows, width), bf16),
            jax.ShapeDtypeStruct((SUB, rows), f32),
        ),
        in_specs=[any_space] * 3 + [vmem] * 3,
        out_specs=(any_space, vmem),
        scratch_shapes=[
            pltpu.VMEM((groups, rows, WIDE), bf16),
            pltpu.VMEM((groups, rows, WIDE), bf16),
            pltpu.VMEM((groups, rows, WIDE), bf16),
            pltpu.VMEM((groups, rows, WIDE), bf16),
            pltpu.VMEM((tiles * ORDER, LANES), f32),
            pltpu.VMEM((tiles * ORDER, LANES), f32),
            pltpu.VMEM((groups, ORDER, SUB, LANES), f32),
            pltpu.VMEM((STEP, SUB, LANES), f32),
            pltpu.VMEM((tiles * rows, LANES), f32),
            pltpu.VMEM((groups, rows, SUB, LANES), f32),
            pltpu.VMEM((groups, rows // STEP, ORDER, SUB, LANES), f32),
            pltpu.VMEM((groups * ORDER, SUB, LANES), f32),
            pltpu.VMEM((n, keep, SUB, LANES), f32),
            pltpu.VMEM((n, keep, SUB, LANES), f32),
            pltpu.VMEM((groups * ORDER, SUB, LANES), f32),
            pltpu.VMEM((rows, LANES), f32),
            pltpu.VMEM((SUB, rows), f32),
            pltpu.VMEM((ntp, SUB, rows), f32),
            dma((groups,)),
            dma((groups,)),
            dma((groups,)),
            dma((groups,)),
            dma((n_own,)),
            dma((n,)),
            dma((n,)),
            dma((n_own,)),
            dma((ntp,)),
            dma((ntp,)),
        ],
        compiler_params=pltpu.CompilerParams(
            collective_id=0,
            has_side_effects=True,
            vmem_limit_bytes=40 * 1024 * 1024,
        ),
        cost_estimate=pl.CostEstimate(
            flops=5 * ORDER * rows * width,
            bytes_accessed=8 * rows * width,
            transcendentals=ORDER * width,
        ),
    )(
        hyena_q,
        hyena_k,
        hyena_v,
        filter_rate.T,
        filter_residue.T,
        skip.reshape(tiles, LANES),
    )
    scale = jnp.sqrt(sums[0] / D + 1e-06)[:, None]
    return (gated.astype(f32) / scale).astype(bf16)


def solution(mesh):
    n, ntp = mesh.shape["ctx"], mesh.shape["tp"]
    in_specs = (
        P("ctx", "tp"),
        P("ctx", "tp"),
        P("ctx", "tp"),
        P("tp", None),
        P("tp", None),
        P("tp"),
    )
    return jax.shard_map(
        functools.partial(per_device, n, ntp),
        mesh=mesh,
        in_specs=in_specs,
        out_specs=P("ctx", "tp"),
        check_vma=False,
    )
```

```python
import functools

import jax
import jax.numpy as jnp
from jax import lax
from jax.experimental import pallas as pl
from jax.experimental.pallas import tpu as pltpu
from jax.sharding import PartitionSpec as P

D = 8192
ORDER = 16
LANES = 128
SUB = 8
WIDE = SUB * LANES
STEP = 16
MESH = pl.DeviceIdType.MESH


def kernel(
    n,
    ntp,
    n_own,
    q_hbm,
    k_hbm,
    v_hbm,
    rate_hbm,
    res_hbm,
    skip_hbm,
    gated_hbm,
    sums_ref,
    qv,
    kv,
    vv,
    gv,
    rate_v,
    res_v,
    skip_v,
    rate_s,
    res_s,
    decay_s,
    block_s,
    pos,
    fir,
    held,
    ends,
    ends_pair,
    chip_ends,
    ends_in,
    carry_out,
    carry_in,
    carry_pair,
    carry,
    squares,
    sums_own,
    sums_in,
    q_sem,
    k_sem,
    v_sem,
    g_sem,
    param_sem,
    pair_send,
    pair_recv,
    end_send,
    end_recv,
    carry_send,
    carry_recv,
    back_send,
    back_recv,
    sum_send,
    sum_recv,
):
    rows, width = q_hbm.shape
    groups = width // WIDE
    blocks = rows // STEP
    tiles = width // LANES
    chips = n // 2
    half = ORDER * groups // 2
    unit = min(ORDER, half)
    units = half // unit
    keep = half // n_own
    spread = chips // n_own
    per_unit = unit // keep
    me = lax.axis_index("ctx")
    me_tp = lax.axis_index("tp")
    chip, core = me // 2, lax.rem(me, 2)
    pair = me + 1 - 2 * core
    own = chip // spread
    first = core * half
    first_pair = half - first
    early = core == 0

    def cols(g):
        return pl.ds(pl.multiple_of(g * WIDE, WIDE), WIDE)

    def load_copy(src, dst, sem, g):
        return pltpu.make_async_copy(src.at[:, cols(g)], dst.at[g], sem.at[g])

    def out_copy(g):
        return pltpu.make_async_copy(gv.at[g], gated_hbm.at[:, cols(g)], g_sem.at[g])

    def param_copy(which):
        src, dst = ((rate_hbm, rate_v), (res_hbm, res_v), (skip_hbm, skip_v))[which]
        return pltpu.make_async_copy(src, dst, param_sem.at[which])

    def first_group(j):
        return lax.rem((1 - core) * (groups // 2) + j, groups)

    def last_group(j):
        return lax.rem(core * (groups // 2) + j, groups)

    def remote(src, dst, send, recv, **where):
        return pltpu.make_async_remote_copy(
            src_ref=src,
            dst_ref=dst,
            send_sem=send,
            recv_sem=recv,
            device_id=where,
            device_id_type=MESH,
        )

    def pair_copy(u):
        return remote(
            ends.at[pl.ds(first_pair + u * unit, unit)],
            ends_pair.at[pl.ds(u * unit, unit)],
            pair_send.at[u],
            pair_recv.at[u],
            ctx=pair,
        )

    def end_copy(owner):
        return remote(
            chip_ends.at[pl.ds(owner * keep, keep)],
            ends_in.at[chip],
            end_send.at[owner],
            end_recv.at[chip],
            ctx=owner * spread * 2 + core,
        )

    def end_arrival(sender):
        return remote(
            chip_ends.at[pl.ds(0, keep)],
            ends_in.at[sender],
            end_send.at[0],
            end_recv.at[sender],
            ctx=sender * 2 + core,
        )

    def carry_copy(target):
        return remote(
            carry_out.at[target],
            carry_in.at[pl.ds(own * keep, keep)],
            carry_send.at[target],
            carry_recv.at[own],
            ctx=target * 2 + core,
        )

    def carry_arrival(owner):
        return remote(
            carry_out.at[0],
            carry_in.at[pl.ds(owner * keep, keep)],
            carry_send.at[0],
            carry_recv.at[owner],
            ctx=owner * spread * 2 + core,
        )

    def back_copy(u):
        return remote(
            carry_pair.at[pl.ds(u * unit, unit)],
            carry.at[pl.ds(first + u * unit, unit)],
            back_send.at[u],
            back_recv.at[u],
            ctx=pair,
        )

    def back_arrival(u):
        return remote(
            carry_pair.at[pl.ds(u * unit, unit)],
            carry.at[pl.ds(first_pair + u * unit, unit)],
            back_send.at[u],
            back_recv.at[u],
            ctx=pair,
        )

    def sum_copy(target):
        return remote(
            sums_own,
            sums_in.at[me_tp],
            sum_send.at[target],
            sum_recv.at[me_tp],
            tp=target,
        )

    def sum_arrival(sender):
        return remote(
            sums_own,
            sums_in.at[sender],
            sum_send.at[0],
            sum_recv.at[sender],
            tp=sender,
        )

    param_copy(0).start()

    def load_group(j, _):
        g = first_group(j)
        load_copy(k_hbm, kv, k_sem, g).start()
        load_copy(v_hbm, vv, v_sem, g).start()
        return 0

    lax.fori_loop(0, groups, load_group, 0)
    param_copy(1).start()
    param_copy(2).start()

    def load_gate(j, _):
        load_copy(q_hbm, qv, q_sem, last_group(j)).start()
        return 0

    lax.fori_loop(0, groups, load_gate, 0)

    barrier = pltpu.get_barrier_semaphore()

    def greet(**where):
        pl.semaphore_signal(barrier, inc=1, device_id=where, device_id_type=MESH)

    def greet_chip(d, _):
        @pl.when(d != chip)
        def _():
            greet(ctx=d * 2 + core)

        return 0

    def greet_tp(d, _):
        @pl.when(d != me_tp)
        def _():
            greet(tp=d)

        return 0

    greet(ctx=pair)
    lax.fori_loop(0, chips, greet_chip, 0)
    lax.fori_loop(0, ntp, greet_tp, 0)

    def spread_tiles(src, dst):
        for tile in range(tiles):
            lanes = slice(tile * LANES, (tile + 1) * LANES)
            dst[tile * ORDER : (tile + 1) * ORDER, :] = src[:, lanes]

    param_copy(0).wait()
    spread_tiles(rate_v, rate_s)

    def mode_row(ref, g, mode):
        return ref[pl.ds(g * (SUB * ORDER) + mode, SUB, stride=ORDER), :]

    def row_power(row, power):
        return jnp.exp(-float(power) * mode_row(rate_s, row // ORDER, row % ORDER))

    def position(g, t):
        return pl.ds(g * (SUB * rows) + t, SUB, stride=rows)

    def tile_rows(g, tile):
        return pl.ds(pl.multiple_of((g * SUB + tile) * rows, rows), rows)

    def chip_unit(u):
        pair_copy(u).wait_recv()
        for r in range(unit):
            row = u * unit + r
            mine, theirs = ends[first + row], ends_pair[row]
            before = jnp.where(early, mine, theirs)
            after = jnp.where(early, theirs, mine)
            chip_ends[row] = before * row_power(first + row, rows) + after
        for part in range(per_unit):
            owner = u * per_unit + part

            @pl.when(owner * spread != chip)
            def _():
                end_copy(owner).start()

    def local_states(j, _):
        g = first_group(j)
        load_copy(k_hbm, kv, k_sem, g).wait()
        load_copy(v_hbm, vv, v_sem, g).wait()
        for tile in range(SUB):
            lanes = slice(tile * LANES, (tile + 1) * LANES)
            wide = kv[g, :, lanes].astype(jnp.float32) * vv[g, :, lanes].astype(
                jnp.float32
            )
            pos[tile_rows(g, tile), :] = wide.astype(jnp.bfloat16).astype(jnp.float32)
        decay = []
        for mode in range(ORDER):
            rate = mode_row(rate_s, g, mode)
            decay.append(jnp.exp(-rate))
            decay_s[g, mode] = decay[mode]
            block_s[mode] = jnp.exp(-float(STEP) * rate)

        def block(b, totals):
            states = [pos[position(g, b * STEP), :]] * ORDER
            for i in range(1, STEP):
                here = pos[position(g, b * STEP + i), :]
                for mode in range(ORDER):
                    states[mode] = states[mode] * decay[mode] + here
            for mode in range(ORDER):
                held[g, b, mode] = states[mode]
            return tuple(
                totals[mode] * block_s[mode] + states[mode] for mode in range(ORDER)
            )

        zero = jnp.zeros((SUB, LANES), jnp.float32)
        totals = lax.fori_loop(0, blocks, block, (zero,) * ORDER)
        for mode in range(ORDER):
            ends[g * ORDER + mode] = totals[mode]

        @pl.when(j == 0)
        def _():
            pl.semaphore_wait(barrier, chips + ntp - 1)

        if groups > 1:

            @pl.when(j < units)
            def _():
                pair_copy(j).start()

            @pl.when(j >= units)
            def _():
                chip_unit(j - units)

        return 0

    lax.fori_loop(0, groups, local_states, 0)
    if groups == 1:
        pair_copy(0).start()
        chip_unit(0)

    param_copy(1).wait()
    param_copy(2).wait()
    spread_tiles(res_v, res_s)

    def near(g, _):
        skip = skip_v[pl.ds(pl.multiple_of(g * SUB, SUB), SUB), :]
        weights = [mode_row(res_s, g, mode) for mode in range(ORDER)]
        taps = []
        for i in range(STEP):
            tap = functools.reduce(lambda x, y: x + y, weights)
            taps.append(tap + skip if i == 0 else tap)
            if i < STEP - 1:
                weights = [weights[mode] * decay_s[g, mode] for mode in range(ORDER)]

        def block(b, _):
            here = [pos[position(g, b * STEP + i), :] for i in range(STEP)]
            for i in range(STEP):
                total = taps[0] * here[i]
                for back in range(1, i + 1):
                    total = total + taps[back] * here[i - back]
                fir[g, b * STEP + i] = total
            for mode in range(ORDER):
                held[g, b, mode] = held[g, b, mode] * mode_row(res_s, g, mode)
            return 0

        lax.fori_loop(0, blocks, block, 0)
        return 0

    lax.fori_loop(0, groups, near, 0)

    def own_scan():
        far = [row_power(first + own * keep + r, 2 * rows) for r in range(keep)]
        ends_in[chip] = chip_ends[pl.ds(own * keep, keep)]

        def one(d, states):
            states = list(states)
            for r in range(keep):
                carry_out[d, r] = states[r]

            @pl.when(d != chip)
            def _():
                carry_copy(d).start()
                end_arrival(d).wait_recv()

            for r in range(keep):
                states[r] = states[r] * far[r] + ends_in[d, r]
            return tuple(states)

        zero = jnp.zeros((SUB, LANES), jnp.float32)
        lax.fori_loop(0, chips, one, (zero,) * keep)
        carry_in[pl.ds(own * keep, keep)] = carry_out[chip]

    if spread == 1:
        own_scan()
    else:
        pl.when(lax.rem(chip, spread) == 0)(own_scan)

    def take_unit(u, _):
        for part in range(per_unit):
            owner = u * per_unit + part

            @pl.when(owner * spread != chip)
            def _():
                carry_arrival(owner).wait_recv()

        for r in range(unit):
            row = u * unit + r
            state = carry_in[row]
            before = jnp.where(early, ends[first + row], ends_pair[row])
            later = state * row_power(first + row, rows) + before
            carry[first + row] = jnp.where(early, state, later)
            carry_pair[row] = jnp.where(early, later, state)
        back_copy(u).start()
        return 0

    lax.fori_loop(0, units, take_unit, 0)

    squares[...] = jnp.zeros_like(squares)

    def finish(j, _):
        g = last_group(j)
        if groups > 1:

            @pl.when(j >= units)
            def _():
                back_arrival(j - units).wait_recv()

        else:
            back_arrival(0).wait_recv()
        decay = [decay_s[g, mode] for mode in range(ORDER)]

        def block(b, terms):
            terms = list(terms)
            for i in range(STEP):
                terms = [terms[mode] * decay[mode] for mode in range(ORDER)]
                tree = [fir[g, b * STEP + i]] + terms
                while len(tree) > 1:
                    pairs = [
                        tree[x] + tree[x + 1] for x in range(0, len(tree) - 1, 2)
                    ]
                    tree = pairs + tree[len(tree) // 2 * 2 :]
                pos[position(g, b * STEP + i), :] = tree[0]
            return tuple(terms[mode] + held[g, b, mode] for mode in range(ORDER))

        start = tuple(
            mode_row(res_s, g, mode) * carry[g * ORDER + mode] for mode in range(ORDER)
        )
        lax.fori_loop(0, blocks, block, start)
        load_copy(q_hbm, qv, q_sem, g).wait()
        for tile in range(SUB):
            lanes = slice(tile * LANES, (tile + 1) * LANES)
            gated = (
                qv[g, :, lanes].astype(jnp.float32) * pos[tile_rows(g, tile), :]
            ).astype(jnp.bfloat16)
            gv[g, :, lanes] = gated
            wide = gated.astype(jnp.float32)
            squares[...] += wide * wide
        out_copy(g).start()
        return 0

    lax.fori_loop(0, groups, finish, 0)

    sums_own[...] = lax.dot_general(
        jnp.ones((SUB, LANES), jnp.float32),
        squares[...],
        (((1,), (1,)), ((), ())),
        precision=lax.Precision.HIGHEST,
        preferred_element_type=jnp.float32,
    )

    def send_sum(d, _):
        @pl.when(d != me_tp)
        def _():
            sum_copy(d).start()

        return 0

    lax.fori_loop(0, ntp, send_sum, 0)
    sums_in[me_tp] = sums_own[...]

    def drain_out(g, _):
        out_copy(g).wait()
        return 0

    lax.fori_loop(0, groups, drain_out, 0)

    def drain_units(u, _):
        pair_copy(u).wait_send()
        back_copy(u).wait_send()
        return 0

    lax.fori_loop(0, units, drain_units, 0)

    def drain_ends(owner, _):
        @pl.when(owner * spread != chip)
        def _():
            end_copy(owner).wait_send()

        return 0

    lax.fori_loop(0, n_own, drain_ends, 0)

    def drain_carry():
        def one(d, _):
            @pl.when(d != chip)
            def _():
                carry_copy(d).wait_send()

            return 0

        lax.fori_loop(0, chips, one, 0)

    if spread == 1:
        drain_carry()
    else:
        pl.when(lax.rem(chip, spread) == 0)(drain_carry)

    def take_sum(d, _):
        @pl.when(d != me_tp)
        def _():
            sum_arrival(d).wait_recv()
            sum_copy(d).wait_send()

        return 0

    lax.fori_loop(0, ntp, take_sum, 0)
    total = sums_in[0]
    for d in range(1, ntp):
        total = total + sums_in[d]
    sums_ref[...] = total


def per_device(n, ntp, hyena_q, hyena_k, hyena_v, filter_rate, filter_residue, skip):
    rows, width = hyena_q.shape
    groups = width // WIDE
    chips = n // 2
    half = ORDER * groups // 2
    units = half // min(ORDER, half)
    n_own = min(chips, half)
    keep = half // n_own
    tiles = width // LANES
    f32, bf16 = jnp.float32, jnp.bfloat16
    any_space = pl.BlockSpec(memory_space=pl.ANY)
    hbm = pl.BlockSpec(memory_space=pltpu.HBM)
    vmem = pl.BlockSpec(memory_space=pltpu.VMEM)
    dma = pltpu.SemaphoreType.DMA
    gated, sums = pl.pallas_call(
        functools.partial(kernel, n, ntp, n_own),
        out_shape=(
            jax.ShapeDtypeStruct((rows, width), bf16),
            jax.ShapeDtypeStruct((SUB, rows), f32),
        ),
        in_specs=[hbm] * 6,
        out_specs=(any_space, vmem),
        scratch_shapes=[
            pltpu.VMEM((groups, rows, WIDE), bf16),
            pltpu.VMEM((groups, rows, WIDE), bf16),
            pltpu.VMEM((groups, rows, WIDE), bf16),
            pltpu.VMEM((groups, rows, WIDE), bf16),
            pltpu.VMEM((ORDER, width), f32),
            pltpu.VMEM((ORDER, width), f32),
            pltpu.VMEM((tiles, LANES), f32),
            pltpu.VMEM((tiles * ORDER, LANES), f32),
            pltpu.VMEM((tiles * ORDER, LANES), f32),
            pltpu.VMEM((groups, ORDER, SUB, LANES), f32),
            pltpu.VMEM((ORDER, SUB, LANES), f32),
            pltpu.VMEM((tiles * rows, LANES), f32),
            pltpu.VMEM((groups, rows, SUB, LANES), f32),
            pltpu.VMEM((groups, rows // STEP, ORDER, SUB, LANES), f32),
            pltpu.VMEM((2 * half, SUB, LANES), f32),
            pltpu.VMEM((half, SUB, LANES), f32),
            pltpu.VMEM((half, SUB, LANES), f32),
            pltpu.VMEM((chips, keep, SUB, LANES), f32),
            pltpu.VMEM((chips, keep, SUB, LANES), f32),
            pltpu.VMEM((half, SUB, LANES), f32),
            pltpu.VMEM((half, SUB, LANES), f32),
            pltpu.VMEM((2 * half, SUB, LANES), f32),
            pltpu.VMEM((rows, LANES), f32),
            pltpu.VMEM((SUB, rows), f32),
            pltpu.VMEM((ntp, SUB, rows), f32),
            dma((groups,)),
            dma((groups,)),
            dma((groups,)),
            dma((groups,)),
            dma((3,)),
            dma((units,)),
            dma((units,)),
            dma((n_own,)),
            dma((chips,)),
            dma((chips,)),
            dma((n_own,)),
            dma((units,)),
            dma((units,)),
            dma((ntp,)),
            dma((ntp,)),
        ],
        compiler_params=pltpu.CompilerParams(
            collective_id=0,
            has_side_effects=True,
            vmem_limit_bytes=40 * 1024 * 1024,
        ),
        cost_estimate=pl.CostEstimate(
            flops=5 * ORDER * rows * width,
            bytes_accessed=8 * rows * width,
            transcendentals=ORDER * width,
        ),
    )(
        hyena_q,
        hyena_k,
        hyena_v,
        filter_rate.T,
        filter_residue.T,
        skip.reshape(tiles, LANES),
    )
    scale = jnp.sqrt(sums[0] / D + 1e-06)[:, None]
    return (gated.astype(f32) / scale).astype(bf16)


def solution(mesh):
    n, ntp = mesh.shape["ctx"], mesh.shape["tp"]
    in_specs = (
        P("ctx", "tp"),
        P("ctx", "tp"),
        P("ctx", "tp"),
        P("tp", None),
        P("tp", None),
        P("tp"),
    )
    return jax.shard_map(
        functools.partial(per_device, n, ntp),
        mesh=mesh,
        in_specs=in_specs,
        out_specs=P("ctx", "tp"),
        check_vma=False,
    )
```

```python
import functools

import jax
import jax.numpy as jnp
from jax import lax
from jax.experimental import pallas as pl
from jax.experimental.pallas import tpu as pltpu
from jax.sharding import PartitionSpec as P

D = 8192
ORDER = 16
LANES = 128
SUB = 8
WIDE = SUB * LANES
STEP = 16
MESH = pl.DeviceIdType.MESH


def kernel(
    n,
    ntp,
    n_own,
    q_hbm,
    k_hbm,
    v_hbm,
    rate_hbm,
    res_hbm,
    skip_hbm,
    gated_hbm,
    sums_ref,
    qv,
    kv,
    vv,
    gv,
    rate_v,
    res_v,
    skip_v,
    rate_s,
    res_s,
    decay_s,
    block_s,
    pos,
    fir,
    held,
    ends,
    ends_pair,
    chip_ends,
    ends_in,
    carry_out,
    carry_in,
    carry_pair,
    carry,
    squares,
    sums_own,
    sums_in,
    q_sem,
    k_sem,
    v_sem,
    g_sem,
    param_sem,
    pair_send,
    pair_recv,
    end_send,
    end_recv,
    carry_send,
    carry_recv,
    back_send,
    back_recv,
    sum_send,
    sum_recv,
):
    rows, width = q_hbm.shape
    groups = width // WIDE
    blocks = rows // STEP
    tiles = width // LANES
    chips = n // 2
    half = ORDER * groups // 2
    unit = min(ORDER, half)
    units = half // unit
    keep = half // n_own
    spread = chips // n_own
    per_unit = unit // keep
    me = lax.axis_index("ctx")
    me_tp = lax.axis_index("tp")
    chip, core = me // 2, lax.rem(me, 2)
    pair = me + 1 - 2 * core
    own = chip // spread
    first = core * half
    first_pair = half - first
    early = core == 0

    def cols(g):
        return pl.ds(pl.multiple_of(g * WIDE, WIDE), WIDE)

    def load_copy(src, dst, sem, g):
        return pltpu.make_async_copy(src.at[:, cols(g)], dst.at[g], sem.at[g])

    def out_copy(g):
        return pltpu.make_async_copy(gv.at[g], gated_hbm.at[:, cols(g)], g_sem.at[g])

    def param_copy(which):
        src, dst = ((rate_hbm, rate_v), (res_hbm, res_v), (skip_hbm, skip_v))[which]
        return pltpu.make_async_copy(src, dst, param_sem.at[which])

    def first_group(j):
        return lax.rem((1 - core) * (groups // 2) + j, groups)

    def last_group(j):
        return lax.rem(core * (groups // 2) + j, groups)

    def remote(src, dst, send, recv, **where):
        return pltpu.make_async_remote_copy(
            src_ref=src,
            dst_ref=dst,
            send_sem=send,
            recv_sem=recv,
            device_id=where,
            device_id_type=MESH,
        )

    def pair_copy(u):
        return remote(
            ends.at[pl.ds(first_pair + u * unit, unit)],
            ends_pair.at[pl.ds(u * unit, unit)],
            pair_send.at[u],
            pair_recv.at[u],
            ctx=pair,
        )

    def end_copy(owner):
        return remote(
            chip_ends.at[pl.ds(owner * keep, keep)],
            ends_in.at[chip],
            end_send.at[owner],
            end_recv.at[chip],
            ctx=owner * spread * 2 + core,
        )

    def end_arrival(sender):
        return remote(
            chip_ends.at[pl.ds(0, keep)],
            ends_in.at[sender],
            end_send.at[0],
            end_recv.at[sender],
            ctx=sender * 2 + core,
        )

    def carry_copy(target):
        return remote(
            carry_out.at[target],
            carry_in.at[pl.ds(own * keep, keep)],
            carry_send.at[target],
            carry_recv.at[own],
            ctx=target * 2 + core,
        )

    def carry_arrival(owner):
        return remote(
            carry_out.at[0],
            carry_in.at[pl.ds(owner * keep, keep)],
            carry_send.at[0],
            carry_recv.at[owner],
            ctx=owner * spread * 2 + core,
        )

    def back_copy(u):
        return remote(
            carry_pair.at[pl.ds(u * unit, unit)],
            carry.at[pl.ds(first + u * unit, unit)],
            back_send.at[u],
            back_recv.at[u],
            ctx=pair,
        )

    def back_arrival(u):
        return remote(
            carry_pair.at[pl.ds(u * unit, unit)],
            carry.at[pl.ds(first_pair + u * unit, unit)],
            back_send.at[u],
            back_recv.at[u],
            ctx=pair,
        )

    def sum_copy(target):
        return remote(
            sums_own,
            sums_in.at[me_tp],
            sum_send.at[target],
            sum_recv.at[me_tp],
            tp=target,
        )

    def sum_arrival(sender):
        return remote(
            sums_own,
            sums_in.at[sender],
            sum_send.at[0],
            sum_recv.at[sender],
            tp=sender,
        )

    param_copy(0).start()

    def load_group(j, _):
        g = first_group(j)
        load_copy(k_hbm, kv, k_sem, g).start()
        load_copy(v_hbm, vv, v_sem, g).start()
        return 0

    lax.fori_loop(0, groups, load_group, 0)
    param_copy(1).start()
    param_copy(2).start()

    def load_gate(j, _):
        load_copy(q_hbm, qv, q_sem, last_group(j)).start()
        return 0

    lax.fori_loop(0, groups, load_gate, 0)

    barrier = pltpu.get_barrier_semaphore()

    def greet(**where):
        pl.semaphore_signal(barrier, inc=1, device_id=where, device_id_type=MESH)

    def greet_chip(d, _):
        @pl.when(d != chip)
        def _():
            greet(ctx=d * 2 + core)

        return 0

    def greet_tp(d, _):
        @pl.when(d != me_tp)
        def _():
            greet(tp=d)

        return 0

    greet(ctx=pair)
    lax.fori_loop(0, chips, greet_chip, 0)
    lax.fori_loop(0, ntp, greet_tp, 0)

    def spread_tiles(src, dst):
        for tile in range(tiles):
            lanes = slice(tile * LANES, (tile + 1) * LANES)
            dst[tile * ORDER : (tile + 1) * ORDER, :] = src[:, lanes]

    param_copy(0).wait()
    spread_tiles(rate_v, rate_s)

    def mode_row(ref, g, mode):
        return ref[pl.ds(g * (SUB * ORDER) + mode, SUB, stride=ORDER), :]

    def row_power(row, power):
        return jnp.exp(-float(power) * mode_row(rate_s, row // ORDER, row % ORDER))

    def position(g, t):
        return pl.ds(g * (SUB * rows) + t, SUB, stride=rows)

    def tile_rows(g, tile):
        return pl.ds(pl.multiple_of((g * SUB + tile) * rows, rows), rows)

    def chip_unit(u):
        pair_copy(u).wait_recv()
        for r in range(unit):
            row = u * unit + r
            mine, theirs = ends[first + row], ends_pair[row]
            before = jnp.where(early, mine, theirs)
            after = jnp.where(early, theirs, mine)
            chip_ends[row] = before * row_power(first + row, rows) + after
        for part in range(per_unit):
            owner = u * per_unit + part

            @pl.when(owner * spread != chip)
            def _():
                end_copy(owner).start()

    def local_states(j, _):
        g = first_group(j)
        load_copy(k_hbm, kv, k_sem, g).wait()
        load_copy(v_hbm, vv, v_sem, g).wait()
        for tile in range(SUB):
            lanes = slice(tile * LANES, (tile + 1) * LANES)
            wide = kv[g, :, lanes].astype(jnp.float32) * vv[g, :, lanes].astype(
                jnp.float32
            )
            pos[tile_rows(g, tile), :] = wide.astype(jnp.bfloat16).astype(jnp.float32)
        decay = []
        for mode in range(ORDER):
            rate = mode_row(rate_s, g, mode)
            decay.append(jnp.exp(-rate))
            decay_s[g, mode] = decay[mode]
            block_s[mode] = jnp.exp(-float(STEP) * rate)

        def block(b, totals):
            states = [pos[position(g, b * STEP), :]] * ORDER
            for i in range(1, STEP):
                here = pos[position(g, b * STEP + i), :]
                for mode in range(ORDER):
                    states[mode] = states[mode] * decay[mode] + here
            for mode in range(ORDER):
                held[g, b, mode] = states[mode]
            return tuple(
                totals[mode] * block_s[mode] + states[mode] for mode in range(ORDER)
            )

        zero = jnp.zeros((SUB, LANES), jnp.float32)
        totals = lax.fori_loop(0, blocks, block, (zero,) * ORDER)
        for mode in range(ORDER):
            ends[g * ORDER + mode] = totals[mode]

        @pl.when(j == 0)
        def _():
            pl.semaphore_wait(barrier, chips + ntp - 1)

        if groups > 1:

            @pl.when(j < units)
            def _():
                pair_copy(j).start()

            @pl.when(j >= units)
            def _():
                chip_unit(j - units)

        return 0

    lax.fori_loop(0, groups, local_states, 0)
    if groups == 1:
        pair_copy(0).start()
        chip_unit(0)

    param_copy(1).wait()
    param_copy(2).wait()
    spread_tiles(res_v, res_s)

    def near(g, _):
        skip = skip_v[pl.ds(pl.multiple_of(g * SUB, SUB), SUB), :]
        weights = [mode_row(res_s, g, mode) for mode in range(ORDER)]
        taps = []
        for i in range(STEP):
            tap = functools.reduce(lambda x, y: x + y, weights)
            taps.append(tap + skip if i == 0 else tap)
            if i < STEP - 1:
                weights = [weights[mode] * decay_s[g, mode] for mode in range(ORDER)]

        def block(b, _):
            here = [pos[position(g, b * STEP + i), :] for i in range(STEP)]
            for i in range(STEP):
                total = taps[0] * here[i]
                for back in range(1, i + 1):
                    total = total + taps[back] * here[i - back]
                fir[g, b * STEP + i] = total
            for mode in range(ORDER):
                held[g, b, mode] = held[g, b, mode] * mode_row(res_s, g, mode)
            return 0

        lax.fori_loop(0, blocks, block, 0)
        return 0

    ahead = (groups + 1) // 2
    lax.fori_loop(0, ahead, near, 0)

    def own_scan():
        far = [row_power(first + own * keep + r, 2 * rows) for r in range(keep)]
        ends_in[chip] = chip_ends[pl.ds(own * keep, keep)]

        def one(d, states):
            states = list(states)
            for r in range(keep):
                carry_out[d, r] = states[r]

            @pl.when(d != chip)
            def _():
                carry_copy(d).start()
                end_arrival(d).wait_recv()

            for r in range(keep):
                states[r] = states[r] * far[r] + ends_in[d, r]
            return tuple(states)

        zero = jnp.zeros((SUB, LANES), jnp.float32)
        lax.fori_loop(0, chips, one, (zero,) * keep)
        carry_in[pl.ds(own * keep, keep)] = carry_out[chip]

    if spread == 1:
        own_scan()
    else:
        pl.when(lax.rem(chip, spread) == 0)(own_scan)

    lax.fori_loop(ahead, groups, near, 0)

    def take_unit(u, _):
        for part in range(per_unit):
            owner = u * per_unit + part

            @pl.when(owner * spread != chip)
            def _():
                carry_arrival(owner).wait_recv()

        for r in range(unit):
            row = u * unit + r
            state = carry_in[row]
            before = jnp.where(early, ends[first + row], ends_pair[row])
            later = state * row_power(first + row, rows) + before
            carry[first + row] = jnp.where(early, state, later)
            carry_pair[row] = jnp.where(early, later, state)
        back_copy(u).start()
        return 0

    lax.fori_loop(0, units, take_unit, 0)

    squares[...] = jnp.zeros_like(squares)

    def finish(j, _):
        g = last_group(j)
        if groups > 1:

            @pl.when(j >= units)
            def _():
                back_arrival(j - units).wait_recv()

        else:
            back_arrival(0).wait_recv()
        decay = [decay_s[g, mode] for mode in range(ORDER)]

        def block(b, terms):
            terms = list(terms)
            for i in range(STEP):
                terms = [terms[mode] * decay[mode] for mode in range(ORDER)]
                tree = [fir[g, b * STEP + i]] + terms
                while len(tree) > 1:
                    pairs = [
                        tree[x] + tree[x + 1] for x in range(0, len(tree) - 1, 2)
                    ]
                    tree = pairs + tree[len(tree) // 2 * 2 :]
                pos[position(g, b * STEP + i), :] = tree[0]
            return tuple(terms[mode] + held[g, b, mode] for mode in range(ORDER))

        start = tuple(
            mode_row(res_s, g, mode) * carry[g * ORDER + mode] for mode in range(ORDER)
        )
        lax.fori_loop(0, blocks, block, start)
        load_copy(q_hbm, qv, q_sem, g).wait()
        for tile in range(SUB):
            lanes = slice(tile * LANES, (tile + 1) * LANES)
            gated = (
                qv[g, :, lanes].astype(jnp.float32) * pos[tile_rows(g, tile), :]
            ).astype(jnp.bfloat16)
            gv[g, :, lanes] = gated
            wide = gated.astype(jnp.float32)
            squares[...] += wide * wide
        out_copy(g).start()
        return 0

    lax.fori_loop(0, groups, finish, 0)

    sums_own[...] = lax.dot_general(
        jnp.ones((SUB, LANES), jnp.float32),
        squares[...],
        (((1,), (1,)), ((), ())),
        precision=lax.Precision.HIGHEST,
        preferred_element_type=jnp.float32,
    )

    def send_sum(d, _):
        @pl.when(d != me_tp)
        def _():
            sum_copy(d).start()

        return 0

    lax.fori_loop(0, ntp, send_sum, 0)
    sums_in[me_tp] = sums_own[...]

    def drain_out(g, _):
        out_copy(g).wait()
        return 0

    lax.fori_loop(0, groups, drain_out, 0)

    def drain_units(u, _):
        pair_copy(u).wait_send()
        back_copy(u).wait_send()
        return 0

    lax.fori_loop(0, units, drain_units, 0)

    def drain_ends(owner, _):
        @pl.when(owner * spread != chip)
        def _():
            end_copy(owner).wait_send()

        return 0

    lax.fori_loop(0, n_own, drain_ends, 0)

    def drain_carry():
        def one(d, _):
            @pl.when(d != chip)
            def _():
                carry_copy(d).wait_send()

            return 0

        lax.fori_loop(0, chips, one, 0)

    if spread == 1:
        drain_carry()
    else:
        pl.when(lax.rem(chip, spread) == 0)(drain_carry)

    def take_sum(d, _):
        @pl.when(d != me_tp)
        def _():
            sum_arrival(d).wait_recv()
            sum_copy(d).wait_send()

        return 0

    lax.fori_loop(0, ntp, take_sum, 0)
    total = sums_in[0]
    for d in range(1, ntp):
        total = total + sums_in[d]
    sums_ref[...] = total


def per_device(n, ntp, hyena_q, hyena_k, hyena_v, filter_rate, filter_residue, skip):
    rows, width = hyena_q.shape
    groups = width // WIDE
    chips = n // 2
    half = ORDER * groups // 2
    units = half // min(ORDER, half)
    n_own = min(chips, half)
    keep = half // n_own
    tiles = width // LANES
    f32, bf16 = jnp.float32, jnp.bfloat16
    any_space = pl.BlockSpec(memory_space=pl.ANY)
    hbm = pl.BlockSpec(memory_space=pltpu.HBM)
    vmem = pl.BlockSpec(memory_space=pltpu.VMEM)
    dma = pltpu.SemaphoreType.DMA
    gated, sums = pl.pallas_call(
        functools.partial(kernel, n, ntp, n_own),
        out_shape=(
            jax.ShapeDtypeStruct((rows, width), bf16),
            jax.ShapeDtypeStruct((SUB, rows), f32),
        ),
        in_specs=[hbm] * 6,
        out_specs=(any_space, vmem),
        scratch_shapes=[
            pltpu.VMEM((groups, rows, WIDE), bf16),
            pltpu.VMEM((groups, rows, WIDE), bf16),
            pltpu.VMEM((groups, rows, WIDE), bf16),
            pltpu.VMEM((groups, rows, WIDE), bf16),
            pltpu.VMEM((ORDER, width), f32),
            pltpu.VMEM((ORDER, width), f32),
            pltpu.VMEM((tiles, LANES), f32),
            pltpu.VMEM((tiles * ORDER, LANES), f32),
            pltpu.VMEM((tiles * ORDER, LANES), f32),
            pltpu.VMEM((groups, ORDER, SUB, LANES), f32),
            pltpu.VMEM((ORDER, SUB, LANES), f32),
            pltpu.VMEM((tiles * rows, LANES), f32),
            pltpu.VMEM((groups, rows, SUB, LANES), f32),
            pltpu.VMEM((groups, rows // STEP, ORDER, SUB, LANES), f32),
            pltpu.VMEM((2 * half, SUB, LANES), f32),
            pltpu.VMEM((half, SUB, LANES), f32),
            pltpu.VMEM((half, SUB, LANES), f32),
            pltpu.VMEM((chips, keep, SUB, LANES), f32),
            pltpu.VMEM((chips, keep, SUB, LANES), f32),
            pltpu.VMEM((half, SUB, LANES), f32),
            pltpu.VMEM((half, SUB, LANES), f32),
            pltpu.VMEM((2 * half, SUB, LANES), f32),
            pltpu.VMEM((rows, LANES), f32),
            pltpu.VMEM((SUB, rows), f32),
            pltpu.VMEM((ntp, SUB, rows), f32),
            dma((groups,)),
            dma((groups,)),
            dma((groups,)),
            dma((groups,)),
            dma((3,)),
            dma((units,)),
            dma((units,)),
            dma((n_own,)),
            dma((chips,)),
            dma((chips,)),
            dma((n_own,)),
            dma((units,)),
            dma((units,)),
            dma((ntp,)),
            dma((ntp,)),
        ],
        compiler_params=pltpu.CompilerParams(
            collective_id=0,
            has_side_effects=True,
            vmem_limit_bytes=64 * 1024 * 1024 - 131072,
        ),
        cost_estimate=pl.CostEstimate(
            flops=5 * ORDER * rows * width,
            bytes_accessed=8 * rows * width,
            transcendentals=ORDER * width,
        ),
    )(
        hyena_q,
        hyena_k,
        hyena_v,
        filter_rate.T,
        filter_residue.T,
        skip.reshape(tiles, LANES),
    )
    scale = jnp.sqrt(sums[0] / D + 1e-06)[:, None]
    return (gated.astype(f32) / scale).astype(bf16)


def solution(mesh):
    n, ntp = mesh.shape["ctx"], mesh.shape["tp"]
    in_specs = (
        P("ctx", "tp"),
        P("ctx", "tp"),
        P("ctx", "tp"),
        P("tp", None),
        P("tp", None),
        P("tp"),
    )
    return jax.shard_map(
        functools.partial(per_device, n, ntp),
        mesh=mesh,
        in_specs=in_specs,
        out_specs=P("ctx", "tp"),
        check_vma=False,
    )
```

```python
import functools

import jax
import jax.numpy as jnp
from jax import lax
from jax.experimental import pallas as pl
from jax.experimental.pallas import tpu as pltpu
from jax.sharding import PartitionSpec as P

D = 8192
ORDER = 16
LANES = 128
SUB = 8
WIDE = SUB * LANES
STEP = 16
MESH = pl.DeviceIdType.MESH


def kernel(
    n,
    ntp,
    n_own,
    q_hbm,
    k_hbm,
    v_hbm,
    rate_hbm,
    res_hbm,
    skip_hbm,
    gated_hbm,
    sums_ref,
    qv,
    kv,
    vv,
    gv,
    rate_v,
    res_v,
    skip_v,
    rate_s,
    res_s,
    decay_s,
    block_s,
    pos,
    fir,
    held,
    ends,
    ends_pair,
    chip_ends,
    ends_in,
    carry_out,
    carry_in,
    carry_pair,
    carry,
    squares,
    sums_own,
    sums_in,
    q_sem,
    k_sem,
    v_sem,
    g_sem,
    param_sem,
    pair_send,
    pair_recv,
    end_send,
    end_recv,
    carry_send,
    carry_recv,
    back_send,
    back_recv,
    sum_send,
    sum_recv,
):
    rows, width = q_hbm.shape
    groups = width // WIDE
    blocks = rows // STEP
    tiles = width // LANES
    chips = n // 2
    half = ORDER * groups // 2
    unit = min(ORDER, half)
    units = half // unit
    keep = unit // n_own
    spread = chips // n_own
    me = lax.axis_index("ctx")
    me_tp = lax.axis_index("tp")
    chip, core = me // 2, lax.rem(me, 2)
    pair = me + 1 - 2 * core
    own = chip // spread
    first = core * half
    first_pair = half - first
    early = core == 0

    def cols(g):
        return pl.ds(pl.multiple_of(g * WIDE, WIDE), WIDE)

    def load_copy(src, dst, sem, g):
        return pltpu.make_async_copy(src.at[:, cols(g)], dst.at[g], sem.at[g])

    def out_copy(g):
        return pltpu.make_async_copy(gv.at[g], gated_hbm.at[:, cols(g)], g_sem.at[g])

    def param_copy(which):
        src, dst = ((rate_hbm, rate_v), (res_hbm, res_v), (skip_hbm, skip_v))[which]
        return pltpu.make_async_copy(src, dst, param_sem.at[which])

    def first_group(j):
        whose = lax.rem(core + 1 + j, 2)
        return lax.rem(whose * (groups // 2) + j // 2, groups)

    def last_group(j):
        return lax.rem(core * (groups // 2) + j, groups)

    def remote(src, dst, send, recv, **where):
        return pltpu.make_async_remote_copy(
            src_ref=src,
            dst_ref=dst,
            send_sem=send,
            recv_sem=recv,
            device_id=where,
            device_id_type=MESH,
        )

    def pair_copy(u):
        return remote(
            ends.at[pl.ds(first_pair + u * unit, unit)],
            ends_pair.at[pl.ds(u * unit, unit)],
            pair_send.at[u],
            pair_recv.at[u],
            ctx=pair,
        )

    def end_copy(u, owner):
        return remote(
            chip_ends.at[pl.ds(u * unit + owner * keep, keep)],
            ends_in.at[u * chips + chip],
            end_send.at[u * n_own + owner],
            end_recv.at[u * chips + chip],
            ctx=owner * spread * 2 + core,
        )

    def end_arrival(u, sender):
        return remote(
            chip_ends.at[pl.ds(0, keep)],
            ends_in.at[u * chips + sender],
            end_send.at[0],
            end_recv.at[u * chips + sender],
            ctx=sender * 2 + core,
        )

    def carry_copy(u, target):
        return remote(
            carry_out.at[u * chips + target],
            carry_in.at[pl.ds(u * unit + own * keep, keep)],
            carry_send.at[u * chips + target],
            carry_recv.at[u * n_own + own],
            ctx=target * 2 + core,
        )

    def carry_arrival(u, owner):
        return remote(
            carry_out.at[0],
            carry_in.at[pl.ds(u * unit + owner * keep, keep)],
            carry_send.at[0],
            carry_recv.at[u * n_own + owner],
            ctx=owner * spread * 2 + core,
        )

    def back_copy(u):
        return remote(
            carry_pair.at[pl.ds(u * unit, unit)],
            carry.at[pl.ds(first + u * unit, unit)],
            back_send.at[u],
            back_recv.at[u],
            ctx=pair,
        )

    def back_arrival(u):
        return remote(
            carry_pair.at[pl.ds(u * unit, unit)],
            carry.at[pl.ds(first_pair + u * unit, unit)],
            back_send.at[u],
            back_recv.at[u],
            ctx=pair,
        )

    def sum_copy(target):
        return remote(
            sums_own,
            sums_in.at[me_tp],
            sum_send.at[target],
            sum_recv.at[me_tp],
            tp=target,
        )

    def sum_arrival(sender):
        return remote(
            sums_own,
            sums_in.at[sender],
            sum_send.at[0],
            sum_recv.at[sender],
            tp=sender,
        )

    param_copy(0).start()

    def load_group(j, _):
        g = first_group(j)
        load_copy(k_hbm, kv, k_sem, g).start()
        load_copy(v_hbm, vv, v_sem, g).start()
        return 0

    lax.fori_loop(0, groups, load_group, 0)
    param_copy(1).start()
    param_copy(2).start()

    def load_gate(j, _):
        load_copy(q_hbm, qv, q_sem, last_group(j)).start()
        return 0

    lax.fori_loop(0, groups, load_gate, 0)

    barrier = pltpu.get_barrier_semaphore()

    def greet(**where):
        pl.semaphore_signal(barrier, inc=1, device_id=where, device_id_type=MESH)

    def greet_chip(d, _):
        @pl.when(d != chip)
        def _():
            greet(ctx=d * 2 + core)

        return 0

    def greet_tp(d, _):
        @pl.when(d != me_tp)
        def _():
            greet(tp=d)

        return 0

    greet(ctx=pair)
    lax.fori_loop(0, chips, greet_chip, 0)
    lax.fori_loop(0, ntp, greet_tp, 0)

    def spread_tiles(src, dst):
        for tile in range(tiles):
            lanes = slice(tile * LANES, (tile + 1) * LANES)
            dst[tile * ORDER : (tile + 1) * ORDER, :] = src[:, lanes]

    param_copy(0).wait()
    spread_tiles(rate_v, rate_s)

    def mode_row(ref, g, mode):
        return ref[pl.ds(g * (SUB * ORDER) + mode, SUB, stride=ORDER), :]

    def row_power(row, power):
        return jnp.exp(-float(power) * mode_row(rate_s, row // ORDER, row % ORDER))

    def position(g, t):
        return pl.ds(g * (SUB * rows) + t, SUB, stride=rows)

    def tile_rows(g, tile):
        return pl.ds(pl.multiple_of((g * SUB + tile) * rows, rows), rows)

    def chip_unit(u):
        pair_copy(u).wait_recv()
        for r in range(unit):
            row = u * unit + r
            mine, theirs = ends[first + row], ends_pair[row]
            before = jnp.where(early, mine, theirs)
            after = jnp.where(early, theirs, mine)
            chip_ends[row] = before * row_power(first + row, rows) + after
        for owner in range(n_own):

            @pl.when(owner * spread != chip)
            def _():
                end_copy(u, owner).start()

    def local_states(j, _):
        g = first_group(j)
        load_copy(k_hbm, kv, k_sem, g).wait()
        load_copy(v_hbm, vv, v_sem, g).wait()
        for tile in range(SUB):
            lanes = slice(tile * LANES, (tile + 1) * LANES)
            wide = kv[g, :, lanes].astype(jnp.float32) * vv[g, :, lanes].astype(
                jnp.float32
            )
            pos[tile_rows(g, tile), :] = wide.astype(jnp.bfloat16).astype(jnp.float32)
        decay = []
        for mode in range(ORDER):
            rate = mode_row(rate_s, g, mode)
            decay.append(jnp.exp(-rate))
            decay_s[g, mode] = decay[mode]
            block_s[mode] = jnp.exp(-float(STEP) * rate)

        def block(b, totals):
            states = [pos[position(g, b * STEP), :]] * ORDER
            for i in range(1, STEP):
                here = pos[position(g, b * STEP + i), :]
                for mode in range(ORDER):
                    states[mode] = states[mode] * decay[mode] + here
            for mode in range(ORDER):
                held[g, b, mode] = states[mode]
            return tuple(
                totals[mode] * block_s[mode] + states[mode] for mode in range(ORDER)
            )

        zero = jnp.zeros((SUB, LANES), jnp.float32)
        totals = lax.fori_loop(0, blocks, block, (zero,) * ORDER)
        for mode in range(ORDER):
            ends[g * ORDER + mode] = totals[mode]

        @pl.when(j == 0)
        def _():
            pl.semaphore_wait(barrier, chips + ntp - 1)

        if groups > 1:

            @pl.when(lax.rem(j, 2) == 0)
            def _():
                pair_copy(j // 2).start()

            @pl.when(lax.rem(j, 2) == 1)
            def _():
                chip_unit(j // 2)

        return 0

    lax.fori_loop(0, groups, local_states, 0)
    if groups == 1:
        pair_copy(0).start()
        chip_unit(0)

    param_copy(1).wait()
    param_copy(2).wait()
    spread_tiles(res_v, res_s)

    def near(g, _):
        skip = skip_v[pl.ds(pl.multiple_of(g * SUB, SUB), SUB), :]
        weights = [mode_row(res_s, g, mode) for mode in range(ORDER)]
        taps = []
        for i in range(STEP):
            tap = functools.reduce(lambda x, y: x + y, weights)
            taps.append(tap + skip if i == 0 else tap)
            if i < STEP - 1:
                weights = [weights[mode] * decay_s[g, mode] for mode in range(ORDER)]

        def block(b, _):
            here = [pos[position(g, b * STEP + i), :] for i in range(STEP)]
            for i in range(STEP):
                total = taps[0] * here[i]
                for back in range(1, i + 1):
                    total = total + taps[back] * here[i - back]
                fir[g, b * STEP + i] = total
            for mode in range(ORDER):
                held[g, b, mode] = held[g, b, mode] * mode_row(res_s, g, mode)
            return 0

        lax.fori_loop(0, blocks, block, 0)
        return 0

    def own_scan(u):
        mine = u * unit + own * keep
        far = [row_power(first + mine + r, 2 * rows) for r in range(keep)]
        ends_in[u * chips + chip] = chip_ends[pl.ds(mine, keep)]

        def one(d, states):
            states = list(states)
            for r in range(keep):
                carry_out[u * chips + d, r] = states[r]

            @pl.when(d != chip)
            def _():
                carry_copy(u, d).start()
                end_arrival(u, d).wait_recv()

            for r in range(keep):
                states[r] = states[r] * far[r] + ends_in[u * chips + d, r]
            return tuple(states)

        zero = jnp.zeros((SUB, LANES), jnp.float32)
        lax.fori_loop(0, chips, one, (zero,) * keep)
        carry_in[pl.ds(mine, keep)] = carry_out[u * chips + chip]

    def scan(u):
        if spread == 1:
            own_scan(u)
        else:
            pl.when(lax.rem(chip, spread) == 0)(lambda: own_scan(u))

    lax.fori_loop(0, 1, near, 0)
    scan(0)
    for u in range(1, units):
        lax.fori_loop(2 * u - 1, 2 * u + 1, near, 0)
        scan(u)
    if groups > 1:
        lax.fori_loop(2 * units - 1, groups, near, 0)

    def take_unit(u):
        for owner in range(n_own):

            @pl.when(owner * spread != chip)
            def _():
                carry_arrival(u, owner).wait_recv()

        for r in range(unit):
            row = u * unit + r
            state = carry_in[row]
            before = jnp.where(early, ends[first + row], ends_pair[row])
            later = state * row_power(first + row, rows) + before
            carry[first + row] = jnp.where(early, state, later)
            carry_pair[row] = jnp.where(early, later, state)
        back_copy(u).start()

    squares[...] = jnp.zeros_like(squares)

    def finish(j, _):
        g = last_group(j)
        if groups > 1:
            pl.when(j < units)(lambda: take_unit(j))

            @pl.when(j >= units)
            def _():
                back_arrival(j - units).wait_recv()

        else:
            take_unit(0)
            back_arrival(0).wait_recv()
        decay = [decay_s[g, mode] for mode in range(ORDER)]

        def block(b, terms):
            terms = list(terms)
            for i in range(STEP):
                terms = [terms[mode] * decay[mode] for mode in range(ORDER)]
                tree = [fir[g, b * STEP + i]] + terms
                while len(tree) > 1:
                    pairs = [
                        tree[x] + tree[x + 1] for x in range(0, len(tree) - 1, 2)
                    ]
                    tree = pairs + tree[len(tree) // 2 * 2 :]
                pos[position(g, b * STEP + i), :] = tree[0]
            return tuple(terms[mode] + held[g, b, mode] for mode in range(ORDER))

        start = tuple(
            mode_row(res_s, g, mode) * carry[g * ORDER + mode] for mode in range(ORDER)
        )
        lax.fori_loop(0, blocks, block, start)
        load_copy(q_hbm, qv, q_sem, g).wait()
        for tile in range(SUB):
            lanes = slice(tile * LANES, (tile + 1) * LANES)
            gated = (
                qv[g, :, lanes].astype(jnp.float32) * pos[tile_rows(g, tile), :]
            ).astype(jnp.bfloat16)
            gv[g, :, lanes] = gated
            wide = gated.astype(jnp.float32)
            squares[...] += wide * wide
        out_copy(g).start()
        return 0

    lax.fori_loop(0, groups, finish, 0)

    sums_own[...] = lax.dot_general(
        jnp.ones((SUB, LANES), jnp.float32),
        squares[...],
        (((1,), (1,)), ((), ())),
        precision=lax.Precision.HIGHEST,
        preferred_element_type=jnp.float32,
    )

    def send_sum(d, _):
        @pl.when(d != me_tp)
        def _():
            sum_copy(d).start()

        return 0

    lax.fori_loop(0, ntp, send_sum, 0)
    sums_in[me_tp] = sums_own[...]

    def drain_out(g, _):
        out_copy(g).wait()
        return 0

    lax.fori_loop(0, groups, drain_out, 0)

    def drain_units(u, _):
        pair_copy(u).wait_send()
        back_copy(u).wait_send()
        return 0

    lax.fori_loop(0, units, drain_units, 0)

    def drain_ends(i, _):
        u, owner = i // n_own, lax.rem(i, n_own)

        @pl.when(owner * spread != chip)
        def _():
            end_copy(u, owner).wait_send()

        return 0

    lax.fori_loop(0, units * n_own, drain_ends, 0)

    def drain_carry():
        def one(i, _):
            u, d = i // chips, lax.rem(i, chips)

            @pl.when(d != chip)
            def _():
                carry_copy(u, d).wait_send()

            return 0

        lax.fori_loop(0, units * chips, one, 0)

    if spread == 1:
        drain_carry()
    else:
        pl.when(lax.rem(chip, spread) == 0)(drain_carry)

    def take_sum(d, _):
        @pl.when(d != me_tp)
        def _():
            sum_arrival(d).wait_recv()
            sum_copy(d).wait_send()

        return 0

    lax.fori_loop(0, ntp, take_sum, 0)
    total = sums_in[0]
    for d in range(1, ntp):
        total = total + sums_in[d]
    sums_ref[...] = total


def normalize(gated_ref, sums_ref, out_ref, scale):
    @pl.when(pl.program_id(0) == 0)
    def _():
        root = jnp.sqrt(sums_ref[0:1, :] / D + 1e-06)
        scale[...] = jnp.broadcast_to(1.0 / root, (LANES, scale.shape[0])).T

    for tile in range(SUB):
        lanes = slice(tile * LANES, (tile + 1) * LANES)
        wide = gated_ref[:, lanes].astype(jnp.float32) * scale[...]
        out_ref[:, lanes] = wide.astype(jnp.bfloat16)


def per_device(n, ntp, hyena_q, hyena_k, hyena_v, filter_rate, filter_residue, skip):
    rows, width = hyena_q.shape
    groups = width // WIDE
    chips = n // 2
    half = ORDER * groups // 2
    unit = min(ORDER, half)
    units = half // unit
    n_own = min(chips, unit)
    keep = unit // n_own
    tiles = width // LANES
    f32, bf16 = jnp.float32, jnp.bfloat16
    any_space = pl.BlockSpec(memory_space=pl.ANY)
    hbm = pl.BlockSpec(memory_space=pltpu.HBM)
    vmem = pl.BlockSpec(memory_space=pltpu.VMEM)
    dma = pltpu.SemaphoreType.DMA
    gated, sums = pl.pallas_call(
        functools.partial(kernel, n, ntp, n_own),
        out_shape=(
            jax.ShapeDtypeStruct((rows, width), bf16),
            jax.ShapeDtypeStruct((SUB, rows), f32),
        ),
        in_specs=[hbm] * 6,
        out_specs=(any_space, vmem),
        scratch_shapes=[
            pltpu.VMEM((groups, rows, WIDE), bf16),
            pltpu.VMEM((groups, rows, WIDE), bf16),
            pltpu.VMEM((groups, rows, WIDE), bf16),
            pltpu.VMEM((groups, rows, WIDE), bf16),
            pltpu.VMEM((ORDER, width), f32),
            pltpu.VMEM((ORDER, width), f32),
            pltpu.VMEM((tiles, LANES), f32),
            pltpu.VMEM((tiles * ORDER, LANES), f32),
            pltpu.VMEM((tiles * ORDER, LANES), f32),
            pltpu.VMEM((groups, ORDER, SUB, LANES), f32),
            pltpu.VMEM((ORDER, SUB, LANES), f32),
            pltpu.VMEM((tiles * rows, LANES), f32),
            pltpu.VMEM((groups, rows, SUB, LANES), f32),
            pltpu.VMEM((groups, rows // STEP, ORDER, SUB, LANES), f32),
            pltpu.VMEM((2 * half, SUB, LANES), f32),
            pltpu.VMEM((half, SUB, LANES), f32),
            pltpu.VMEM((half, SUB, LANES), f32),
            pltpu.VMEM((units * chips, keep, SUB, LANES), f32),
            pltpu.VMEM((units * chips, keep, SUB, LANES), f32),
            pltpu.VMEM((half, SUB, LANES), f32),
            pltpu.VMEM((half, SUB, LANES), f32),
            pltpu.VMEM((2 * half, SUB, LANES), f32),
            pltpu.VMEM((rows, LANES), f32),
            pltpu.VMEM((SUB, rows), f32),
            pltpu.VMEM((ntp, SUB, rows), f32),
            dma((groups,)),
            dma((groups,)),
            dma((groups,)),
            dma((groups,)),
            dma((3,)),
            dma((units,)),
            dma((units,)),
            dma((units * n_own,)),
            dma((units * chips,)),
            dma((units * chips,)),
            dma((units * n_own,)),
            dma((units,)),
            dma((units,)),
            dma((ntp,)),
            dma((ntp,)),
        ],
        compiler_params=pltpu.CompilerParams(
            collective_id=0,
            has_side_effects=True,
            vmem_limit_bytes=64 * 1024 * 1024 - 131072,
        ),
        cost_estimate=pl.CostEstimate(
            flops=5 * ORDER * rows * width,
            bytes_accessed=8 * rows * width,
            transcendentals=ORDER * width,
        ),
    )(
        hyena_q,
        hyena_k,
        hyena_v,
        filter_rate.T,
        filter_residue.T,
        skip.reshape(tiles, LANES),
    )
    return pl.pallas_call(
        normalize,
        out_shape=jax.ShapeDtypeStruct((rows, width), bf16),
        grid=(groups,),
        in_specs=[
            pl.BlockSpec((rows, WIDE), lambda j: (0, j)),
            pl.BlockSpec((SUB, rows), lambda j: (0, 0)),
        ],
        out_specs=pl.BlockSpec((rows, WIDE), lambda j: (0, j)),
        scratch_shapes=[pltpu.VMEM((rows, LANES), f32)],
        compiler_params=pltpu.CompilerParams(
            vmem_limit_bytes=64 * 1024 * 1024 - 131072
        ),
    )(gated, sums)


def solution(mesh):
    n, ntp = mesh.shape["ctx"], mesh.shape["tp"]
    in_specs = (
        P("ctx", "tp"),
        P("ctx", "tp"),
        P("ctx", "tp"),
        P("tp", None),
        P("tp", None),
        P("tp"),
    )
    return jax.shard_map(
        functools.partial(per_device, n, ntp),
        mesh=mesh,
        in_specs=in_specs,
        out_specs=P("ctx", "tp"),
        check_vma=False,
    )
```

```python
import functools

import jax
import jax.numpy as jnp
from jax import lax
from jax.experimental import pallas as pl
from jax.experimental.pallas import tpu as pltpu
from jax.sharding import PartitionSpec as P

D = 8192
ORDER = 16
LANES = 128
SUB = 8
WIDE = SUB * LANES
STEP = 16
MESH = pl.DeviceIdType.MESH


def kernel(
    n,
    ntp,
    n_own,
    q_hbm,
    k_hbm,
    v_hbm,
    rate_hbm,
    res_hbm,
    skip_hbm,
    gated_hbm,
    sums_ref,
    qv,
    kv,
    vv,
    gv,
    rate_v,
    res_v,
    skip_v,
    rate_s,
    res_s,
    decay_s,
    block_s,
    pos,
    fir,
    held,
    ends,
    ends_pair,
    chip_ends,
    ends_in,
    carry_out,
    carry_in,
    carry_pair,
    carry,
    squares,
    sums_own,
    sums_in,
    q_sem,
    k_sem,
    v_sem,
    g_sem,
    param_sem,
    pair_send,
    pair_recv,
    end_send,
    end_recv,
    carry_send,
    carry_recv,
    back_send,
    back_recv,
    sum_send,
    sum_recv,
):
    rows, width = q_hbm.shape
    groups = width // WIDE
    blocks = rows // STEP
    tiles = width // LANES
    chips = n // 2
    half = ORDER * groups // 2
    unit = min(ORDER, half)
    units = half // unit
    keep = unit // n_own
    spread = chips // n_own
    me = lax.axis_index("ctx")
    me_tp = lax.axis_index("tp")
    chip, core = me // 2, lax.rem(me, 2)
    pair = me + 1 - 2 * core
    own = chip // spread
    first = core * half
    first_pair = half - first
    early = core == 0

    def cols(g):
        return pl.ds(pl.multiple_of(g * WIDE, WIDE), WIDE)

    def load_copy(src, dst, sem, g):
        return pltpu.make_async_copy(src.at[:, cols(g)], dst.at[g], sem.at[g])

    def out_copy(g):
        return pltpu.make_async_copy(gv.at[g], gated_hbm.at[:, cols(g)], g_sem.at[g])

    def param_copy(which):
        src, dst = ((rate_hbm, rate_v), (res_hbm, res_v), (skip_hbm, skip_v))[which]
        return pltpu.make_async_copy(src, dst, param_sem.at[which])

    def first_group(j):
        whose = lax.rem(core + 1 + j, 2)
        return lax.rem(whose * (groups // 2) + j // 2, groups)

    def last_group(j):
        return lax.rem(core * (groups // 2) + j, groups)

    def remote(src, dst, send, recv, **where):
        return pltpu.make_async_remote_copy(
            src_ref=src,
            dst_ref=dst,
            send_sem=send,
            recv_sem=recv,
            device_id=where,
            device_id_type=MESH,
        )

    def pair_copy(u):
        return remote(
            ends.at[pl.ds(first_pair + u * unit, unit)],
            ends_pair.at[pl.ds(u * unit, unit)],
            pair_send.at[u],
            pair_recv.at[u],
            ctx=pair,
        )

    def end_copy(u, owner):
        return remote(
            chip_ends.at[pl.ds(u * unit + owner * keep, keep)],
            ends_in.at[u * chips + chip],
            end_send.at[u * n_own + owner],
            end_recv.at[u * chips + chip],
            ctx=owner * spread * 2 + core,
        )

    def end_arrival(u, sender):
        return remote(
            chip_ends.at[pl.ds(0, keep)],
            ends_in.at[u * chips + sender],
            end_send.at[0],
            end_recv.at[u * chips + sender],
            ctx=sender * 2 + core,
        )

    def carry_copy(u, target):
        return remote(
            carry_out.at[u * chips + target],
            carry_in.at[pl.ds(u * unit + own * keep, keep)],
            carry_send.at[u * chips + target],
            carry_recv.at[u * n_own + own],
            ctx=target * 2 + core,
        )

    def carry_arrival(u, owner):
        return remote(
            carry_out.at[0],
            carry_in.at[pl.ds(u * unit + owner * keep, keep)],
            carry_send.at[0],
            carry_recv.at[u * n_own + owner],
            ctx=owner * spread * 2 + core,
        )

    def back_copy(u):
        return remote(
            carry_pair.at[pl.ds(u * unit, unit)],
            carry.at[pl.ds(first + u * unit, unit)],
            back_send.at[u],
            back_recv.at[u],
            ctx=pair,
        )

    def back_arrival(u):
        return remote(
            carry_pair.at[pl.ds(u * unit, unit)],
            carry.at[pl.ds(first_pair + u * unit, unit)],
            back_send.at[u],
            back_recv.at[u],
            ctx=pair,
        )

    def sum_copy(target):
        return remote(
            sums_own,
            sums_in.at[me_tp],
            sum_send.at[target],
            sum_recv.at[me_tp],
            tp=target,
        )

    def sum_arrival(sender):
        return remote(
            sums_own,
            sums_in.at[sender],
            sum_send.at[0],
            sum_recv.at[sender],
            tp=sender,
        )

    param_copy(0).start()

    def load_group(j, _):
        g = first_group(j)
        load_copy(k_hbm, kv, k_sem, g).start()
        load_copy(v_hbm, vv, v_sem, g).start()
        return 0

    lax.fori_loop(0, groups, load_group, 0)
    param_copy(1).start()
    param_copy(2).start()

    def load_gate(j, _):
        load_copy(q_hbm, qv, q_sem, last_group(j)).start()
        return 0

    lax.fori_loop(0, groups, load_gate, 0)

    barrier = pltpu.get_barrier_semaphore()

    def greet(**where):
        pl.semaphore_signal(barrier, inc=1, device_id=where, device_id_type=MESH)

    def greet_chip(d, _):
        @pl.when(d != chip)
        def _():
            greet(ctx=d * 2 + core)

        return 0

    def greet_tp(d, _):
        @pl.when(d != me_tp)
        def _():
            greet(tp=d)

        return 0

    greet(ctx=pair)
    lax.fori_loop(0, chips, greet_chip, 0)
    lax.fori_loop(0, ntp, greet_tp, 0)

    def spread_tiles(src, dst):
        for tile in range(tiles):
            lanes = slice(tile * LANES, (tile + 1) * LANES)
            dst[pl.ds(tile * (ORDER + 1), ORDER), :] = src[:, lanes]

    param_copy(0).wait()
    spread_tiles(rate_v, rate_s)

    def mode_row(ref, g, mode):
        pitch = ORDER + 1
        return ref[pl.ds(g * (SUB * pitch) + mode, SUB, stride=pitch), :]

    def row_power(row, power):
        return jnp.exp(-float(power) * mode_row(rate_s, row // ORDER, row % ORDER))

    def position(g, t):
        return pl.ds(g * (SUB * (rows + 1)) + t, SUB, stride=rows + 1)

    def tile_rows(g, tile):
        return pl.ds((g * SUB + tile) * (rows + 1), rows)

    def chip_unit(u):
        pair_copy(u).wait_recv()
        for r in range(unit):
            row = u * unit + r
            mine, theirs = ends[first + row], ends_pair[row]
            before = jnp.where(early, mine, theirs)
            after = jnp.where(early, theirs, mine)
            chip_ends[row] = before * row_power(first + row, rows) + after
        for owner in range(n_own):

            @pl.when(owner * spread != chip)
            def _():
                end_copy(u, owner).start()

    def local_states(j, _):
        g = first_group(j)
        load_copy(k_hbm, kv, k_sem, g).wait()
        load_copy(v_hbm, vv, v_sem, g).wait()
        for tile in range(SUB):
            lanes = slice(tile * LANES, (tile + 1) * LANES)
            wide = kv[g, :, lanes].astype(jnp.float32) * vv[g, :, lanes].astype(
                jnp.float32
            )
            pos[tile_rows(g, tile), :] = wide.astype(jnp.bfloat16).astype(jnp.float32)
        decay = []
        for mode in range(ORDER):
            rate = mode_row(rate_s, g, mode)
            decay.append(jnp.exp(-rate))
            decay_s[g, mode] = decay[mode]
            block_s[mode] = jnp.exp(-float(STEP) * rate)

        def block(b, totals):
            states = [pos[position(g, b * STEP), :]] * ORDER
            for i in range(1, STEP):
                here = pos[position(g, b * STEP + i), :]
                for mode in range(ORDER):
                    states[mode] = states[mode] * decay[mode] + here
            for mode in range(ORDER):
                held[g, b, mode] = states[mode]
            return tuple(
                totals[mode] * block_s[mode] + states[mode] for mode in range(ORDER)
            )

        zero = jnp.zeros((SUB, LANES), jnp.float32)
        totals = lax.fori_loop(0, blocks, block, (zero,) * ORDER)
        for mode in range(ORDER):
            ends[g * ORDER + mode] = totals[mode]

        @pl.when(j == 0)
        def _():
            pl.semaphore_wait(barrier, chips + ntp - 1)

        if groups > 1:

            @pl.when(lax.rem(j, 2) == 0)
            def _():
                pair_copy(j // 2).start()

            @pl.when(lax.rem(j, 2) == 1)
            def _():
                chip_unit(j // 2)

        return 0

    lax.fori_loop(0, groups, local_states, 0)
    if groups == 1:
        pair_copy(0).start()
        chip_unit(0)

    param_copy(1).wait()
    param_copy(2).wait()
    spread_tiles(res_v, res_s)

    def near(g, _):
        skip = skip_v[pl.ds(pl.multiple_of(g * SUB, SUB), SUB), :]
        weights = [mode_row(res_s, g, mode) for mode in range(ORDER)]
        taps = []
        for i in range(STEP):
            tap = functools.reduce(lambda x, y: x + y, weights)
            taps.append(tap + skip if i == 0 else tap)
            if i < STEP - 1:
                weights = [weights[mode] * decay_s[g, mode] for mode in range(ORDER)]

        def block(b, _):
            here = [pos[position(g, b * STEP + i), :] for i in range(STEP)]
            for i in range(STEP):
                total = taps[0] * here[i]
                for back in range(1, i + 1):
                    total = total + taps[back] * here[i - back]
                fir[g, b * STEP + i] = total
            for mode in range(ORDER):
                held[g, b, mode] = held[g, b, mode] * mode_row(res_s, g, mode)
            return 0

        lax.fori_loop(0, blocks, block, 0)
        return 0

    def own_scan(u):
        mine = u * unit + own * keep
        far = [row_power(first + mine + r, 2 * rows) for r in range(keep)]
        ends_in[u * chips + chip] = chip_ends[pl.ds(mine, keep)]

        def one(d, states):
            states = list(states)
            for r in range(keep):
                carry_out[u * chips + d, r] = states[r]

            @pl.when(d != chip)
            def _():
                carry_copy(u, d).start()
                end_arrival(u, d).wait_recv()

            for r in range(keep):
                states[r] = states[r] * far[r] + ends_in[u * chips + d, r]
            return tuple(states)

        zero = jnp.zeros((SUB, LANES), jnp.float32)
        lax.fori_loop(0, chips, one, (zero,) * keep)
        carry_in[pl.ds(mine, keep)] = carry_out[u * chips + chip]

    def scan(u):
        if spread == 1:
            own_scan(u)
        else:
            pl.when(lax.rem(chip, spread) == 0)(lambda: own_scan(u))

    lax.fori_loop(0, 1, near, 0)
    scan(0)
    for u in range(1, units):
        lax.fori_loop(2 * u - 1, 2 * u + 1, near, 0)
        scan(u)
    if groups > 1:
        lax.fori_loop(2 * units - 1, groups, near, 0)

    def take_unit(u):
        for owner in range(n_own):

            @pl.when(owner * spread != chip)
            def _():
                carry_arrival(u, owner).wait_recv()

        for r in range(unit):
            row = u * unit + r
            state = carry_in[row]
            before = jnp.where(early, ends[first + row], ends_pair[row])
            later = state * row_power(first + row, rows) + before
            carry[first + row] = jnp.where(early, state, later)
            carry_pair[row] = jnp.where(early, later, state)
        back_copy(u).start()

    squares[...] = jnp.zeros_like(squares)

    def finish(j, _):
        g = last_group(j)
        if groups > 1:
            pl.when(j < units)(lambda: take_unit(j))

            @pl.when(j >= units)
            def _():
                back_arrival(j - units).wait_recv()

        else:
            take_unit(0)
            back_arrival(0).wait_recv()
        decay = [decay_s[g, mode] for mode in range(ORDER)]

        def block(b, terms):
            terms = list(terms)
            for i in range(STEP):
                terms = [terms[mode] * decay[mode] for mode in range(ORDER)]
                tree = [fir[g, b * STEP + i]] + terms
                while len(tree) > 1:
                    pairs = [
                        tree[x] + tree[x + 1] for x in range(0, len(tree) - 1, 2)
                    ]
                    tree = pairs + tree[len(tree) // 2 * 2 :]
                pos[position(g, b * STEP + i), :] = tree[0]
            return tuple(terms[mode] + held[g, b, mode] for mode in range(ORDER))

        start = tuple(
            mode_row(res_s, g, mode) * carry[g * ORDER + mode] for mode in range(ORDER)
        )
        lax.fori_loop(0, blocks, block, start)
        load_copy(q_hbm, qv, q_sem, g).wait()
        for tile in range(SUB):
            lanes = slice(tile * LANES, (tile + 1) * LANES)
            gated = (
                qv[g, :, lanes].astype(jnp.float32) * pos[tile_rows(g, tile), :]
            ).astype(jnp.bfloat16)
            gv[g, :, lanes] = gated
            wide = gated.astype(jnp.float32)
            squares[...] += wide * wide
        out_copy(g).start()
        return 0

    lax.fori_loop(0, groups, finish, 0)

    sums_own[...] = lax.dot_general(
        jnp.ones((SUB, LANES), jnp.float32),
        squares[...],
        (((1,), (1,)), ((), ())),
        precision=lax.Precision.HIGHEST,
        preferred_element_type=jnp.float32,
    )

    def send_sum(d, _):
        @pl.when(d != me_tp)
        def _():
            sum_copy(d).start()

        return 0

    lax.fori_loop(0, ntp, send_sum, 0)
    sums_in[me_tp] = sums_own[...]

    def drain_out(g, _):
        out_copy(g).wait()
        return 0

    lax.fori_loop(0, groups, drain_out, 0)

    def drain_units(u, _):
        pair_copy(u).wait_send()
        back_copy(u).wait_send()
        return 0

    lax.fori_loop(0, units, drain_units, 0)

    def drain_ends(i, _):
        u, owner = i // n_own, lax.rem(i, n_own)

        @pl.when(owner * spread != chip)
        def _():
            end_copy(u, owner).wait_send()

        return 0

    lax.fori_loop(0, units * n_own, drain_ends, 0)

    def drain_carry():
        def one(i, _):
            u, d = i // chips, lax.rem(i, chips)

            @pl.when(d != chip)
            def _():
                carry_copy(u, d).wait_send()

            return 0

        lax.fori_loop(0, units * chips, one, 0)

    if spread == 1:
        drain_carry()
    else:
        pl.when(lax.rem(chip, spread) == 0)(drain_carry)

    def take_sum(d, _):
        @pl.when(d != me_tp)
        def _():
            sum_arrival(d).wait_recv()
            sum_copy(d).wait_send()

        return 0

    lax.fori_loop(0, ntp, take_sum, 0)
    total = sums_in[0]
    for d in range(1, ntp):
        total = total + sums_in[d]
    sums_ref[...] = total


def normalize(gated_hbm, sums_hbm, out_hbm, gv, ov, sums, scale, g_sem, o_sem, s_sem):
    groups = gv.shape[0]

    def part(j):
        return slice(j * WIDE, (j + 1) * WIDE)

    take = pltpu.make_async_copy(sums_hbm, sums, s_sem)
    take.start()
    reads = [
        pltpu.make_async_copy(gated_hbm.at[:, part(j)], gv.at[j], g_sem.at[j])
        for j in range(groups)
    ]
    writes = [
        pltpu.make_async_copy(ov.at[j], out_hbm.at[:, part(j)], o_sem.at[j])
        for j in range(groups)
    ]
    for read in reads:
        read.start()
    take.wait()
    root = jnp.sqrt(sums[0:1, :] / D + 1e-06)
    scale[...] = jnp.broadcast_to(1.0 / root, (LANES, scale.shape[0])).T
    for j in range(groups):
        reads[j].wait()
        for tile in range(SUB):
            lanes = slice(tile * LANES, (tile + 1) * LANES)
            wide = gv[j, :, lanes].astype(jnp.float32) * scale[...]
            ov[j, :, lanes] = wide.astype(jnp.bfloat16)
        writes[j].start()
    for write in writes:
        write.wait()


def per_device(n, ntp, hyena_q, hyena_k, hyena_v, filter_rate, filter_residue, skip):
    rows, width = hyena_q.shape
    groups = width // WIDE
    chips = n // 2
    half = ORDER * groups // 2
    unit = min(ORDER, half)
    units = half // unit
    n_own = min(chips, unit)
    keep = unit // n_own
    tiles = width // LANES
    f32, bf16 = jnp.float32, jnp.bfloat16
    any_space = pl.BlockSpec(memory_space=pl.ANY)
    hbm = pl.BlockSpec(memory_space=pltpu.HBM)
    vmem = pl.BlockSpec(memory_space=pltpu.VMEM)
    dma = pltpu.SemaphoreType.DMA
    gated, sums = pl.pallas_call(
        functools.partial(kernel, n, ntp, n_own),
        out_shape=(
            jax.ShapeDtypeStruct((rows, width), bf16),
            jax.ShapeDtypeStruct((SUB, rows), f32),
        ),
        in_specs=[hbm] * 6,
        out_specs=(any_space, vmem),
        scratch_shapes=[
            pltpu.VMEM((groups, rows, WIDE), bf16),
            pltpu.VMEM((groups, rows, WIDE), bf16),
            pltpu.VMEM((groups, rows, WIDE), bf16),
            pltpu.VMEM((groups, rows, WIDE), bf16),
            pltpu.VMEM((ORDER, width), f32),
            pltpu.VMEM((ORDER, width), f32),
            pltpu.VMEM((tiles, LANES), f32),
            pltpu.VMEM(((tiles + 1) * (ORDER + 1), LANES), f32),
            pltpu.VMEM(((tiles + 1) * (ORDER + 1), LANES), f32),
            pltpu.VMEM((groups, ORDER, SUB, LANES), f32),
            pltpu.VMEM((ORDER, SUB, LANES), f32),
            pltpu.VMEM(((tiles + 1) * (rows + 1), LANES), f32),
            pltpu.VMEM((groups, rows, SUB, LANES), f32),
            pltpu.VMEM((groups, rows // STEP, ORDER, SUB, LANES), f32),
            pltpu.VMEM((2 * half, SUB, LANES), f32),
            pltpu.VMEM((half, SUB, LANES), f32),
            pltpu.VMEM((half, SUB, LANES), f32),
            pltpu.VMEM((units * chips, keep, SUB, LANES), f32),
            pltpu.VMEM((units * chips, keep, SUB, LANES), f32),
            pltpu.VMEM((half, SUB, LANES), f32),
            pltpu.VMEM((half, SUB, LANES), f32),
            pltpu.VMEM((2 * half, SUB, LANES), f32),
            pltpu.VMEM((rows, LANES), f32),
            pltpu.VMEM((SUB, rows), f32),
            pltpu.VMEM((ntp, SUB, rows), f32),
            dma((groups,)),
            dma((groups,)),
            dma((groups,)),
            dma((groups,)),
            dma((3,)),
            dma((units,)),
            dma((units,)),
            dma((units * n_own,)),
            dma((units * chips,)),
            dma((units * chips,)),
            dma((units * n_own,)),
            dma((units,)),
            dma((units,)),
            dma((ntp,)),
            dma((ntp,)),
        ],
        compiler_params=pltpu.CompilerParams(
            collective_id=0,
            has_side_effects=True,
            vmem_limit_bytes=64 * 1024 * 1024 - 131072,
        ),
        cost_estimate=pl.CostEstimate(
            flops=5 * ORDER * rows * width,
            bytes_accessed=8 * rows * width,
            transcendentals=ORDER * width,
        ),
    )(
        hyena_q,
        hyena_k,
        hyena_v,
        filter_rate.T,
        filter_residue.T,
        skip.reshape(tiles, LANES),
    )
    return pl.pallas_call(
        normalize,
        out_shape=jax.ShapeDtypeStruct((rows, width), bf16),
        in_specs=[any_space, any_space],
        out_specs=any_space,
        scratch_shapes=[
            pltpu.VMEM((groups, rows, WIDE), bf16),
            pltpu.VMEM((groups, rows, WIDE), bf16),
            pltpu.VMEM((SUB, rows), f32),
            pltpu.VMEM((rows, LANES), f32),
            dma((groups,)),
            dma((groups,)),
            dma(()),
        ],
        compiler_params=pltpu.CompilerParams(
            vmem_limit_bytes=64 * 1024 * 1024 - 131072
        ),
    )(gated, sums)


def solution(mesh):
    n, ntp = mesh.shape["ctx"], mesh.shape["tp"]
    in_specs = (
        P("ctx", "tp"),
        P("ctx", "tp"),
        P("ctx", "tp"),
        P("tp", None),
        P("tp", None),
        P("tp"),
    )
    return jax.shard_map(
        functools.partial(per_device, n, ntp),
        mesh=mesh,
        in_specs=in_specs,
        out_specs=P("ctx", "tp"),
        check_vma=False,
    )
```

```python
import functools

import jax
import jax.numpy as jnp
from jax import lax
from jax.experimental import pallas as pl
from jax.experimental.pallas import tpu as pltpu
from jax.sharding import PartitionSpec as P

D = 8192
ORDER = 16
LANES = 128
SUB = 8
WIDE = SUB * LANES
STEP = 16
MESH = pl.DeviceIdType.MESH


def kernel(
    n,
    ntp,
    n_own,
    q_hbm,
    k_hbm,
    v_hbm,
    rate_hbm,
    res_hbm,
    skip_hbm,
    gated_hbm,
    sums_ref,
    qv,
    kv,
    vv,
    gv,
    rate_v,
    res_v,
    skip_v,
    rate_s,
    res_s,
    decay_s,
    block_s,
    pos,
    fir,
    held,
    ends,
    ends_pair,
    chip_ends,
    ends_in,
    carry_out,
    carry_in,
    carry_pair,
    carry,
    squares,
    sums_own,
    sums_in,
    q_sem,
    k_sem,
    v_sem,
    g_sem,
    param_sem,
    pair_send,
    pair_recv,
    end_send,
    end_recv,
    carry_send,
    carry_recv,
    back_send,
    back_recv,
    sum_send,
    sum_recv,
):
    rows, width = q_hbm.shape
    groups = width // WIDE
    blocks = rows // STEP
    tiles = width // LANES
    chips = n // 2
    half = ORDER * groups // 2
    unit = min(ORDER, half)
    units = half // unit
    keep = unit // n_own
    spread = chips // n_own
    me = lax.axis_index("ctx")
    me_tp = lax.axis_index("tp")
    chip, core = me // 2, lax.rem(me, 2)
    pair = me + 1 - 2 * core
    own = chip // spread
    first = core * half
    first_pair = half - first
    early = core == 0

    def cols(g):
        return pl.ds(pl.multiple_of(g * WIDE, WIDE), WIDE)

    def load_copy(src, dst, sem, g):
        return pltpu.make_async_copy(src.at[:, cols(g)], dst.at[g], sem.at[g])

    def out_copy(g):
        return pltpu.make_async_copy(gv.at[g], gated_hbm.at[:, cols(g)], g_sem.at[g])

    def param_copy(which):
        src, dst = ((rate_hbm, rate_v), (res_hbm, res_v), (skip_hbm, skip_v))[which]
        return pltpu.make_async_copy(src, dst, param_sem.at[which])

    def first_group(j):
        whose = lax.rem(core + 1 + j, 2)
        return lax.rem(whose * (groups // 2) + j // 2, groups)

    def last_group(j):
        return lax.rem(core * (groups // 2) + j, groups)

    def remote(src, dst, send, recv, **where):
        return pltpu.make_async_remote_copy(
            src_ref=src,
            dst_ref=dst,
            send_sem=send,
            recv_sem=recv,
            device_id=where,
            device_id_type=MESH,
        )

    def pair_copy(u):
        return remote(
            ends.at[pl.ds(first_pair + u * unit, unit)],
            ends_pair.at[pl.ds(u * unit, unit)],
            pair_send.at[u],
            pair_recv.at[u],
            ctx=pair,
        )

    def end_copy(u, owner):
        return remote(
            chip_ends.at[pl.ds(u * unit + owner * keep, keep)],
            ends_in.at[u * chips + chip],
            end_send.at[u * n_own + owner],
            end_recv.at[u * chips + chip],
            ctx=owner * spread * 2 + core,
        )

    def end_arrival(u, sender):
        return remote(
            chip_ends.at[pl.ds(0, keep)],
            ends_in.at[u * chips + sender],
            end_send.at[0],
            end_recv.at[u * chips + sender],
            ctx=sender * 2 + core,
        )

    def carry_copy(u, target):
        return remote(
            carry_out.at[u * chips + target],
            carry_in.at[pl.ds(u * unit + own * keep, keep)],
            carry_send.at[u * chips + target],
            carry_recv.at[u * n_own + own],
            ctx=target * 2 + core,
        )

    def carry_arrival(u, owner):
        return remote(
            carry_out.at[0],
            carry_in.at[pl.ds(u * unit + owner * keep, keep)],
            carry_send.at[0],
            carry_recv.at[u * n_own + owner],
            ctx=owner * spread * 2 + core,
        )

    def back_copy(u):
        return remote(
            carry_pair.at[pl.ds(u * unit, unit)],
            carry.at[pl.ds(first + u * unit, unit)],
            back_send.at[u],
            back_recv.at[u],
            ctx=pair,
        )

    def back_arrival(u):
        return remote(
            carry_pair.at[pl.ds(u * unit, unit)],
            carry.at[pl.ds(first_pair + u * unit, unit)],
            back_send.at[u],
            back_recv.at[u],
            ctx=pair,
        )

    def sum_copy(target):
        return remote(
            sums_own,
            sums_in.at[me_tp],
            sum_send.at[target],
            sum_recv.at[me_tp],
            tp=target,
        )

    def sum_arrival(sender):
        return remote(
            sums_own,
            sums_in.at[sender],
            sum_send.at[0],
            sum_recv.at[sender],
            tp=sender,
        )

    param_copy(0).start()

    def load_group(j, _):
        g = first_group(j)
        load_copy(k_hbm, kv, k_sem, g).start()
        load_copy(v_hbm, vv, v_sem, g).start()
        return 0

    lax.fori_loop(0, groups, load_group, 0)
    param_copy(1).start()
    param_copy(2).start()

    def load_gate(j, _):
        load_copy(q_hbm, qv, q_sem, last_group(j)).start()
        return 0

    lax.fori_loop(0, groups, load_gate, 0)

    barrier = pltpu.get_barrier_semaphore()

    def greet(**where):
        pl.semaphore_signal(barrier, inc=1, device_id=where, device_id_type=MESH)

    def greet_chip(d, _):
        @pl.when(d != chip)
        def _():
            greet(ctx=d * 2 + core)

        return 0

    def greet_tp(d, _):
        @pl.when(d != me_tp)
        def _():
            greet(tp=d)

        return 0

    greet(ctx=pair)
    lax.fori_loop(0, chips, greet_chip, 0)
    lax.fori_loop(0, ntp, greet_tp, 0)

    def spread_tiles(src, dst):
        for tile in range(tiles):
            lanes = slice(tile * LANES, (tile + 1) * LANES)
            dst[pl.ds(tile * (ORDER + 1), ORDER), :] = src[:, lanes]

    param_copy(0).wait()
    spread_tiles(rate_v, rate_s)

    def mode_row(ref, g, mode):
        pitch = ORDER + 1
        return ref[pl.ds(g * (SUB * pitch) + mode, SUB, stride=pitch), :]

    def row_power(row, power):
        return jnp.exp(-float(power) * mode_row(rate_s, row // ORDER, row % ORDER))

    def position(g, t):
        return pl.ds(g * (SUB * (rows + 1)) + t, SUB, stride=rows + 1)

    def tile_rows(g, tile):
        return pl.ds((g * SUB + tile) * (rows + 1), rows)

    def chip_unit(u):
        pair_copy(u).wait_recv()
        for r in range(unit):
            row = u * unit + r
            mine, theirs = ends[first + row], ends_pair[row]
            before = jnp.where(early, mine, theirs)
            after = jnp.where(early, theirs, mine)
            chip_ends[row] = before * row_power(first + row, rows) + after
        for owner in range(n_own):

            @pl.when(owner * spread != chip)
            def _():
                end_copy(u, owner).start()

    def local_states(j, _):
        g = first_group(j)
        load_copy(k_hbm, kv, k_sem, g).wait()
        load_copy(v_hbm, vv, v_sem, g).wait()
        for tile in range(SUB):
            lanes = slice(tile * LANES, (tile + 1) * LANES)
            wide = kv[g, :, lanes].astype(jnp.float32) * vv[g, :, lanes].astype(
                jnp.float32
            )
            pos[tile_rows(g, tile), :] = wide.astype(jnp.bfloat16).astype(jnp.float32)
        decay = []
        for mode in range(ORDER):
            rate = mode_row(rate_s, g, mode)
            decay.append(jnp.exp(-rate))
            decay_s[g, mode] = decay[mode]
            block_s[mode] = jnp.exp(-float(STEP) * rate)

        def block(b, totals):
            states = [pos[position(g, b * STEP), :]] * ORDER
            for i in range(1, STEP):
                here = pos[position(g, b * STEP + i), :]
                for mode in range(ORDER):
                    states[mode] = states[mode] * decay[mode] + here
            for mode in range(ORDER):
                held[g, b, mode] = states[mode]
            return tuple(
                totals[mode] * block_s[mode] + states[mode] for mode in range(ORDER)
            )

        zero = jnp.zeros((SUB, LANES), jnp.float32)
        totals = lax.fori_loop(0, blocks, block, (zero,) * ORDER)
        for mode in range(ORDER):
            ends[g * ORDER + mode] = totals[mode]

        @pl.when(j == 0)
        def _():
            pl.semaphore_wait(barrier, chips + ntp - 1)

        if groups > 1:

            @pl.when(lax.rem(j, 2) == 0)
            def _():
                pair_copy(j // 2).start()

            @pl.when(lax.rem(j, 2) == 1)
            def _():
                chip_unit(j // 2)

        return 0

    lax.fori_loop(0, groups, local_states, 0)
    if groups == 1:
        pair_copy(0).start()
        chip_unit(0)

    param_copy(1).wait()
    param_copy(2).wait()
    spread_tiles(res_v, res_s)

    def near(g, _):
        skip = skip_v[pl.ds(pl.multiple_of(g * SUB, SUB), SUB), :]
        weights = [mode_row(res_s, g, mode) for mode in range(ORDER)]
        taps = []
        for i in range(STEP):
            tap = functools.reduce(lambda x, y: x + y, weights)
            taps.append(tap + skip if i == 0 else tap)
            if i < STEP - 1:
                weights = [weights[mode] * decay_s[g, mode] for mode in range(ORDER)]

        def block(b, _):
            here = [pos[position(g, b * STEP + i), :] for i in range(STEP)]
            for i in range(STEP):
                total = taps[0] * here[i]
                for back in range(1, i + 1):
                    total = total + taps[back] * here[i - back]
                fir[g, b * STEP + i] = total
            for mode in range(ORDER):
                held[g, b, mode] = held[g, b, mode] * mode_row(res_s, g, mode)
            return 0

        lax.fori_loop(0, blocks, block, 0)
        return 0

    def own_scan(u):
        mine = u * unit + own * keep
        far = [row_power(first + mine + r, 2 * rows) for r in range(keep)]
        ends_in[u * chips + chip] = chip_ends[pl.ds(mine, keep)]

        def one(d, states):
            states = list(states)
            for r in range(keep):
                carry_out[u * chips + d, r] = states[r]

            @pl.when(d != chip)
            def _():
                carry_copy(u, d).start()
                end_arrival(u, d).wait_recv()

            for r in range(keep):
                states[r] = states[r] * far[r] + ends_in[u * chips + d, r]
            return tuple(states)

        zero = jnp.zeros((SUB, LANES), jnp.float32)
        lax.fori_loop(0, chips, one, (zero,) * keep)
        carry_in[pl.ds(mine, keep)] = carry_out[u * chips + chip]

    def scan(u):
        if spread == 1:
            own_scan(u)
        else:
            pl.when(lax.rem(chip, spread) == 0)(lambda: own_scan(u))

    lax.fori_loop(0, 1, near, 0)
    scan(0)
    for u in range(1, units):
        lax.fori_loop(u, u + 1, near, 0)
        scan(u)
    if groups > 1:
        lax.fori_loop(units, groups, near, 0)

    def take_unit(u):
        for owner in range(n_own):

            @pl.when(owner * spread != chip)
            def _():
                carry_arrival(u, owner).wait_recv()

        for r in range(unit):
            row = u * unit + r
            state = carry_in[row]
            before = jnp.where(early, ends[first + row], ends_pair[row])
            later = state * row_power(first + row, rows) + before
            carry[first + row] = jnp.where(early, state, later)
            carry_pair[row] = jnp.where(early, later, state)
        back_copy(u).start()

    squares[...] = jnp.zeros_like(squares)

    def finish(j, _):
        g = last_group(j)
        if groups > 1:
            pl.when(j < units)(lambda: take_unit(j))

            @pl.when(j >= units)
            def _():
                back_arrival(j - units).wait_recv()

        else:
            take_unit(0)
            back_arrival(0).wait_recv()
        decay = [decay_s[g, mode] for mode in range(ORDER)]

        def block(b, terms):
            terms = list(terms)
            for i in range(STEP):
                terms = [terms[mode] * decay[mode] for mode in range(ORDER)]
                tree = [fir[g, b * STEP + i]] + terms
                while len(tree) > 1:
                    pairs = [
                        tree[x] + tree[x + 1] for x in range(0, len(tree) - 1, 2)
                    ]
                    tree = pairs + tree[len(tree) // 2 * 2 :]
                pos[position(g, b * STEP + i), :] = tree[0]
            return tuple(terms[mode] + held[g, b, mode] for mode in range(ORDER))

        start = tuple(
            mode_row(res_s, g, mode) * carry[g * ORDER + mode] for mode in range(ORDER)
        )
        lax.fori_loop(0, blocks, block, start)
        load_copy(q_hbm, qv, q_sem, g).wait()
        for tile in range(SUB):
            lanes = slice(tile * LANES, (tile + 1) * LANES)
            gated = (
                qv[g, :, lanes].astype(jnp.float32) * pos[tile_rows(g, tile), :]
            ).astype(jnp.bfloat16)
            gv[g, :, lanes] = gated
            wide = gated.astype(jnp.float32)
            squares[...] += wide * wide
        out_copy(g).start()
        return 0

    lax.fori_loop(0, groups, finish, 0)

    sums_own[...] = lax.dot_general(
        jnp.ones((SUB, LANES), jnp.float32),
        squares[...],
        (((1,), (1,)), ((), ())),
        precision=lax.Precision.HIGHEST,
        preferred_element_type=jnp.float32,
    )

    def send_sum(d, _):
        @pl.when(d != me_tp)
        def _():
            sum_copy(d).start()

        return 0

    lax.fori_loop(0, ntp, send_sum, 0)
    sums_in[me_tp] = sums_own[...]

    def drain_out(g, _):
        out_copy(g).wait()
        return 0

    lax.fori_loop(0, groups, drain_out, 0)

    def drain_units(u, _):
        pair_copy(u).wait_send()
        back_copy(u).wait_send()
        return 0

    lax.fori_loop(0, units, drain_units, 0)

    def drain_ends(i, _):
        u, owner = i // n_own, lax.rem(i, n_own)

        @pl.when(owner * spread != chip)
        def _():
            end_copy(u, owner).wait_send()

        return 0

    lax.fori_loop(0, units * n_own, drain_ends, 0)

    def drain_carry():
        def one(i, _):
            u, d = i // chips, lax.rem(i, chips)

            @pl.when(d != chip)
            def _():
                carry_copy(u, d).wait_send()

            return 0

        lax.fori_loop(0, units * chips, one, 0)

    if spread == 1:
        drain_carry()
    else:
        pl.when(lax.rem(chip, spread) == 0)(drain_carry)

    def take_sum(d, _):
        @pl.when(d != me_tp)
        def _():
            sum_arrival(d).wait_recv()
            sum_copy(d).wait_send()

        return 0

    lax.fori_loop(0, ntp, take_sum, 0)
    total = sums_in[0]
    for d in range(1, ntp):
        total = total + sums_in[d]
    sums_ref[...] = total


def normalize(gated_hbm, sums_hbm, out_hbm, gv, ov, sums, scale, g_sem, o_sem, s_sem):
    groups = gv.shape[0]

    def part(j):
        return slice(j * WIDE, (j + 1) * WIDE)

    take = pltpu.make_async_copy(sums_hbm, sums, s_sem)
    take.start()
    reads = [
        pltpu.make_async_copy(gated_hbm.at[:, part(j)], gv.at[j], g_sem.at[j])
        for j in range(groups)
    ]
    writes = [
        pltpu.make_async_copy(ov.at[j], out_hbm.at[:, part(j)], o_sem.at[j])
        for j in range(groups)
    ]
    for read in reads:
        read.start()
    take.wait()
    root = jnp.sqrt(sums[0:1, :] / D + 1e-06)
    scale[...] = jnp.broadcast_to(1.0 / root, (LANES, scale.shape[0])).T
    for j in range(groups):
        reads[j].wait()
        for tile in range(SUB):
            lanes = slice(tile * LANES, (tile + 1) * LANES)
            wide = gv[j, :, lanes].astype(jnp.float32) * scale[...]
            ov[j, :, lanes] = wide.astype(jnp.bfloat16)
        writes[j].start()
    for write in writes:
        write.wait()


def per_device(n, ntp, hyena_q, hyena_k, hyena_v, filter_rate, filter_residue, skip):
    rows, width = hyena_q.shape
    groups = width // WIDE
    chips = n // 2
    half = ORDER * groups // 2
    unit = min(ORDER, half)
    units = half // unit
    n_own = min(chips, unit)
    keep = unit // n_own
    tiles = width // LANES
    f32, bf16 = jnp.float32, jnp.bfloat16
    any_space = pl.BlockSpec(memory_space=pl.ANY)
    hbm = pl.BlockSpec(memory_space=pltpu.HBM)
    vmem = pl.BlockSpec(memory_space=pltpu.VMEM)
    dma = pltpu.SemaphoreType.DMA
    gated, sums = pl.pallas_call(
        functools.partial(kernel, n, ntp, n_own),
        out_shape=(
            jax.ShapeDtypeStruct((rows, width), bf16),
            jax.ShapeDtypeStruct((SUB, rows), f32),
        ),
        in_specs=[hbm] * 6,
        out_specs=(any_space, vmem),
        scratch_shapes=[
            pltpu.VMEM((groups, rows, WIDE), bf16),
            pltpu.VMEM((groups, rows, WIDE), bf16),
            pltpu.VMEM((groups, rows, WIDE), bf16),
            pltpu.VMEM((groups, rows, WIDE), bf16),
            pltpu.VMEM((ORDER, width), f32),
            pltpu.VMEM((ORDER, width), f32),
            pltpu.VMEM((tiles, LANES), f32),
            pltpu.VMEM(((tiles + 1) * (ORDER + 1), LANES), f32),
            pltpu.VMEM(((tiles + 1) * (ORDER + 1), LANES), f32),
            pltpu.VMEM((groups, ORDER, SUB, LANES), f32),
            pltpu.VMEM((ORDER, SUB, LANES), f32),
            pltpu.VMEM(((tiles + 1) * (rows + 1), LANES), f32),
            pltpu.VMEM((groups, rows, SUB, LANES), f32),
            pltpu.VMEM((groups, rows // STEP, ORDER, SUB, LANES), f32),
            pltpu.VMEM((2 * half, SUB, LANES), f32),
            pltpu.VMEM((half, SUB, LANES), f32),
            pltpu.VMEM((half, SUB, LANES), f32),
            pltpu.VMEM((units * chips, keep, SUB, LANES), f32),
            pltpu.VMEM((units * chips, keep, SUB, LANES), f32),
            pltpu.VMEM((half, SUB, LANES), f32),
            pltpu.VMEM((half, SUB, LANES), f32),
            pltpu.VMEM((2 * half, SUB, LANES), f32),
            pltpu.VMEM((rows, LANES), f32),
            pltpu.VMEM((SUB, rows), f32),
            pltpu.VMEM((ntp, SUB, rows), f32),
            dma((groups,)),
            dma((groups,)),
            dma((groups,)),
            dma((groups,)),
            dma((3,)),
            dma((units,)),
            dma((units,)),
            dma((units * n_own,)),
            dma((units * chips,)),
            dma((units * chips,)),
            dma((units * n_own,)),
            dma((units,)),
            dma((units,)),
            dma((ntp,)),
            dma((ntp,)),
        ],
        compiler_params=pltpu.CompilerParams(
            collective_id=0,
            has_side_effects=True,
            vmem_limit_bytes=64 * 1024 * 1024 - 131072,
        ),
        cost_estimate=pl.CostEstimate(
            flops=5 * ORDER * rows * width,
            bytes_accessed=8 * rows * width,
            transcendentals=ORDER * width,
        ),
    )(
        hyena_q,
        hyena_k,
        hyena_v,
        filter_rate.T,
        filter_residue.T,
        skip.reshape(tiles, LANES),
    )
    return pl.pallas_call(
        normalize,
        out_shape=jax.ShapeDtypeStruct((rows, width), bf16),
        in_specs=[any_space, any_space],
        out_specs=any_space,
        scratch_shapes=[
            pltpu.VMEM((groups, rows, WIDE), bf16),
            pltpu.VMEM((groups, rows, WIDE), bf16),
            pltpu.VMEM((SUB, rows), f32),
            pltpu.VMEM((rows, LANES), f32),
            dma((groups,)),
            dma((groups,)),
            dma(()),
        ],
        compiler_params=pltpu.CompilerParams(
            vmem_limit_bytes=64 * 1024 * 1024 - 131072
        ),
    )(gated, sums)


def solution(mesh):
    n, ntp = mesh.shape["ctx"], mesh.shape["tp"]
    in_specs = (
        P("ctx", "tp"),
        P("ctx", "tp"),
        P("ctx", "tp"),
        P("tp", None),
        P("tp", None),
        P("tp"),
    )
    return jax.shard_map(
        functools.partial(per_device, n, ntp),
        mesh=mesh,
        in_specs=in_specs,
        out_specs=P("ctx", "tp"),
        check_vma=False,
    )
```

```python
import functools

import jax
import jax.numpy as jnp
from jax import lax
from jax.experimental import pallas as pl
from jax.experimental.pallas import tpu as pltpu
from jax.sharding import PartitionSpec as P

D = 8192
ORDER = 16
LANES = 128
SUB = 8
WIDE = SUB * LANES
STEP = 8
MESH = pl.DeviceIdType.MESH


def kernel(
    n,
    ntp,
    n_own,
    q_hbm,
    k_hbm,
    v_hbm,
    rate_hbm,
    res_hbm,
    skip_hbm,
    gated_hbm,
    sums_ref,
    qv,
    kv,
    vv,
    gv,
    rate_v,
    res_v,
    skip_v,
    rate_s,
    res_s,
    decay_s,
    block_s,
    pos,
    fir,
    held,
    ends,
    ends_pair,
    chip_ends,
    ends_in,
    carry_out,
    carry_in,
    carry_pair,
    carry,
    squares,
    sums_own,
    sums_in,
    q_sem,
    k_sem,
    v_sem,
    g_sem,
    param_sem,
    pair_send,
    pair_recv,
    end_send,
    end_recv,
    carry_send,
    carry_recv,
    back_send,
    back_recv,
    sum_send,
    sum_recv,
):
    rows, width = q_hbm.shape
    groups = width // WIDE
    blocks = rows // STEP
    tiles = width // LANES
    chips = n // 2
    half = ORDER * groups // 2
    unit = min(ORDER, half)
    units = half // unit
    keep = unit // n_own
    spread = chips // n_own
    me = lax.axis_index("ctx")
    me_tp = lax.axis_index("tp")
    chip, core = me // 2, lax.rem(me, 2)
    pair = me + 1 - 2 * core
    own = chip // spread
    first = core * half
    first_pair = half - first
    early = core == 0

    def cols(g):
        return pl.ds(pl.multiple_of(g * WIDE, WIDE), WIDE)

    def load_copy(src, dst, sem, g):
        return pltpu.make_async_copy(src.at[:, cols(g)], dst.at[g], sem.at[g])

    def out_copy(g):
        return pltpu.make_async_copy(gv.at[g], gated_hbm.at[:, cols(g)], g_sem.at[g])

    def param_copy(which):
        src, dst = ((rate_hbm, rate_v), (res_hbm, res_v), (skip_hbm, skip_v))[which]
        return pltpu.make_async_copy(src, dst, param_sem.at[which])

    def first_group(j):
        whose = lax.rem(core + 1 + j, 2)
        return lax.rem(whose * (groups // 2) + j // 2, groups)

    def last_group(j):
        return lax.rem(core * (groups // 2) + j, groups)

    def remote(src, dst, send, recv, **where):
        return pltpu.make_async_remote_copy(
            src_ref=src,
            dst_ref=dst,
            send_sem=send,
            recv_sem=recv,
            device_id=where,
            device_id_type=MESH,
        )

    def pair_copy(u):
        return remote(
            ends.at[pl.ds(first_pair + u * unit, unit)],
            ends_pair.at[pl.ds(u * unit, unit)],
            pair_send.at[u],
            pair_recv.at[u],
            ctx=pair,
        )

    def end_copy(u, owner):
        return remote(
            chip_ends.at[pl.ds(u * unit + owner * keep, keep)],
            ends_in.at[u * chips + chip],
            end_send.at[u * n_own + owner],
            end_recv.at[u * chips + chip],
            ctx=owner * spread * 2 + core,
        )

    def end_arrival(u, sender):
        return remote(
            chip_ends.at[pl.ds(0, keep)],
            ends_in.at[u * chips + sender],
            end_send.at[0],
            end_recv.at[u * chips + sender],
            ctx=sender * 2 + core,
        )

    def carry_copy(u, target):
        return remote(
            carry_out.at[u * chips + target],
            carry_in.at[pl.ds(u * unit + own * keep, keep)],
            carry_send.at[u * chips + target],
            carry_recv.at[u * n_own + own],
            ctx=target * 2 + core,
        )

    def carry_arrival(u, owner):
        return remote(
            carry_out.at[0],
            carry_in.at[pl.ds(u * unit + owner * keep, keep)],
            carry_send.at[0],
            carry_recv.at[u * n_own + owner],
            ctx=owner * spread * 2 + core,
        )

    def back_copy(u):
        return remote(
            carry_pair.at[pl.ds(u * unit, unit)],
            carry.at[pl.ds(first + u * unit, unit)],
            back_send.at[u],
            back_recv.at[u],
            ctx=pair,
        )

    def back_arrival(u):
        return remote(
            carry_pair.at[pl.ds(u * unit, unit)],
            carry.at[pl.ds(first_pair + u * unit, unit)],
            back_send.at[u],
            back_recv.at[u],
            ctx=pair,
        )

    def sum_copy(target):
        return remote(
            sums_own,
            sums_in.at[me_tp],
            sum_send.at[target],
            sum_recv.at[me_tp],
            tp=target,
        )

    def sum_arrival(sender):
        return remote(
            sums_own,
            sums_in.at[sender],
            sum_send.at[0],
            sum_recv.at[sender],
            tp=sender,
        )

    param_copy(0).start()

    def load_group(j, _):
        g = first_group(j)
        load_copy(k_hbm, kv, k_sem, g).start()
        load_copy(v_hbm, vv, v_sem, g).start()
        return 0

    lax.fori_loop(0, groups, load_group, 0)
    param_copy(1).start()
    param_copy(2).start()

    def load_gate(j, _):
        load_copy(q_hbm, qv, q_sem, last_group(j)).start()
        return 0

    lax.fori_loop(0, groups, load_gate, 0)

    barrier = pltpu.get_barrier_semaphore()

    def greet(**where):
        pl.semaphore_signal(barrier, inc=1, device_id=where, device_id_type=MESH)

    def greet_chip(d, _):
        @pl.when(d != chip)
        def _():
            greet(ctx=d * 2 + core)

        return 0

    def greet_tp(d, _):
        @pl.when(d != me_tp)
        def _():
            greet(tp=d)

        return 0

    greet(ctx=pair)
    lax.fori_loop(0, chips, greet_chip, 0)
    lax.fori_loop(0, ntp, greet_tp, 0)

    def spread_tiles(src, dst):
        for tile in range(tiles):
            lanes = slice(tile * LANES, (tile + 1) * LANES)
            dst[pl.ds(tile * (ORDER + 1), ORDER), :] = src[:, lanes]

    param_copy(0).wait()
    spread_tiles(rate_v, rate_s)

    def mode_row(ref, g, mode):
        pitch = ORDER + 1
        return ref[pl.ds(g * (SUB * pitch) + mode, SUB, stride=pitch), :]

    def row_power(row, power):
        return jnp.exp(-float(power) * mode_row(rate_s, row // ORDER, row % ORDER))

    def position(g, t):
        return pl.ds(g * (SUB * (rows + 1)) + t, SUB, stride=rows + 1)

    def tile_rows(g, tile):
        return pl.ds((g * SUB + tile) * (rows + 1), rows)

    def chip_unit(u):
        pair_copy(u).wait_recv()
        for r in range(unit):
            row = u * unit + r
            mine, theirs = ends[first + row], ends_pair[row]
            before = jnp.where(early, mine, theirs)
            after = jnp.where(early, theirs, mine)
            chip_ends[row] = before * row_power(first + row, rows) + after
        for owner in range(n_own):

            @pl.when(owner * spread != chip)
            def _():
                end_copy(u, owner).start()

    def local_states(j, _):
        g = first_group(j)
        load_copy(k_hbm, kv, k_sem, g).wait()
        load_copy(v_hbm, vv, v_sem, g).wait()
        for tile in range(SUB):
            lanes = slice(tile * LANES, (tile + 1) * LANES)
            wide = kv[g, :, lanes].astype(jnp.float32) * vv[g, :, lanes].astype(
                jnp.float32
            )
            pos[tile_rows(g, tile), :] = wide.astype(jnp.bfloat16).astype(jnp.float32)
        decay = []
        for mode in range(ORDER):
            rate = mode_row(rate_s, g, mode)
            decay.append(jnp.exp(-rate))
            decay_s[g, mode] = decay[mode]
            block_s[mode] = jnp.exp(-float(STEP) * rate)

        def block(b, totals):
            states = [pos[position(g, b * STEP), :]] * ORDER
            for i in range(1, STEP):
                here = pos[position(g, b * STEP + i), :]
                for mode in range(ORDER):
                    states[mode] = states[mode] * decay[mode] + here
            for mode in range(ORDER):
                held[g, b, mode] = states[mode]
            return tuple(
                totals[mode] * block_s[mode] + states[mode] for mode in range(ORDER)
            )

        zero = jnp.zeros((SUB, LANES), jnp.float32)
        totals = lax.fori_loop(0, blocks, block, (zero,) * ORDER)
        for mode in range(ORDER):
            ends[g * ORDER + mode] = totals[mode]

        @pl.when(j == 0)
        def _():
            pl.semaphore_wait(barrier, chips + ntp - 1)

        if groups > 1:

            @pl.when(lax.rem(j, 2) == 0)
            def _():
                pair_copy(j // 2).start()

            @pl.when(lax.rem(j, 2) == 1)
            def _():
                chip_unit(j // 2)

        return 0

    lax.fori_loop(0, groups, local_states, 0)
    if groups == 1:
        pair_copy(0).start()
        chip_unit(0)

    param_copy(1).wait()
    param_copy(2).wait()
    spread_tiles(res_v, res_s)

    def near(g, _):
        skip = skip_v[pl.ds(pl.multiple_of(g * SUB, SUB), SUB), :]
        weights = [mode_row(res_s, g, mode) for mode in range(ORDER)]
        taps = []
        for i in range(STEP):
            tap = functools.reduce(lambda x, y: x + y, weights)
            taps.append(tap + skip if i == 0 else tap)
            if i < STEP - 1:
                weights = [weights[mode] * decay_s[g, mode] for mode in range(ORDER)]

        def block(b, _):
            here = [pos[position(g, b * STEP + i), :] for i in range(STEP)]
            for i in range(STEP):
                total = taps[0] * here[i]
                for back in range(1, i + 1):
                    total = total + taps[back] * here[i - back]
                fir[g, b * STEP + i] = total
            for mode in range(ORDER):
                held[g, b, mode] = held[g, b, mode] * mode_row(res_s, g, mode)
            return 0

        lax.fori_loop(0, blocks, block, 0)
        return 0

    def own_scan(u):
        mine = u * unit + own * keep
        far = [row_power(first + mine + r, 2 * rows) for r in range(keep)]
        ends_in[u * chips + chip] = chip_ends[pl.ds(mine, keep)]

        def one(d, states):
            states = list(states)
            for r in range(keep):
                carry_out[u * chips + d, r] = states[r]

            @pl.when(d != chip)
            def _():
                carry_copy(u, d).start()
                end_arrival(u, d).wait_recv()

            for r in range(keep):
                states[r] = states[r] * far[r] + ends_in[u * chips + d, r]
            return tuple(states)

        zero = jnp.zeros((SUB, LANES), jnp.float32)
        lax.fori_loop(0, chips, one, (zero,) * keep)
        carry_in[pl.ds(mine, keep)] = carry_out[u * chips + chip]

    def scan(u):
        if spread == 1:
            own_scan(u)
        else:
            pl.when(lax.rem(chip, spread) == 0)(lambda: own_scan(u))

    lax.fori_loop(0, 1, near, 0)
    scan(0)
    for u in range(1, units):
        lax.fori_loop(u, u + 1, near, 0)
        scan(u)
    if groups > 1:
        lax.fori_loop(units, groups, near, 0)

    def take_unit(u):
        for owner in range(n_own):

            @pl.when(owner * spread != chip)
            def _():
                carry_arrival(u, owner).wait_recv()

        for r in range(unit):
            row = u * unit + r
            state = carry_in[row]
            before = jnp.where(early, ends[first + row], ends_pair[row])
            later = state * row_power(first + row, rows) + before
            carry[first + row] = jnp.where(early, state, later)
            carry_pair[row] = jnp.where(early, later, state)
        back_copy(u).start()

    squares[...] = jnp.zeros_like(squares)

    def finish(j, _):
        g = last_group(j)
        if groups > 1:
            pl.when(j < units)(lambda: take_unit(j))

            @pl.when(j >= units)
            def _():
                back_arrival(j - units).wait_recv()

        else:
            take_unit(0)
            back_arrival(0).wait_recv()
        decay = [decay_s[g, mode] for mode in range(ORDER)]

        def block(b, terms):
            terms = list(terms)
            for i in range(STEP):
                terms = [terms[mode] * decay[mode] for mode in range(ORDER)]
                tree = [fir[g, b * STEP + i]] + terms
                while len(tree) > 1:
                    pairs = [
                        tree[x] + tree[x + 1] for x in range(0, len(tree) - 1, 2)
                    ]
                    tree = pairs + tree[len(tree) // 2 * 2 :]
                pos[position(g, b * STEP + i), :] = tree[0]
            return tuple(terms[mode] + held[g, b, mode] for mode in range(ORDER))

        start = tuple(
            mode_row(res_s, g, mode) * carry[g * ORDER + mode] for mode in range(ORDER)
        )
        lax.fori_loop(0, blocks, block, start)
        load_copy(q_hbm, qv, q_sem, g).wait()
        for tile in range(SUB):
            lanes = slice(tile * LANES, (tile + 1) * LANES)
            gated = (
                qv[g, :, lanes].astype(jnp.float32) * pos[tile_rows(g, tile), :]
            ).astype(jnp.bfloat16)
            gv[g, :, lanes] = gated
            wide = gated.astype(jnp.float32)
            squares[...] += wide * wide
        out_copy(g).start()
        return 0

    lax.fori_loop(0, groups, finish, 0)

    sums_own[...] = lax.dot_general(
        jnp.ones((SUB, LANES), jnp.float32),
        squares[...],
        (((1,), (1,)), ((), ())),
        precision=lax.Precision.HIGHEST,
        preferred_element_type=jnp.float32,
    )

    def send_sum(d, _):
        @pl.when(d != me_tp)
        def _():
            sum_copy(d).start()

        return 0

    lax.fori_loop(0, ntp, send_sum, 0)
    sums_in[me_tp] = sums_own[...]

    def drain_out(g, _):
        out_copy(g).wait()
        return 0

    lax.fori_loop(0, groups, drain_out, 0)

    def drain_units(u, _):
        pair_copy(u).wait_send()
        back_copy(u).wait_send()
        return 0

    lax.fori_loop(0, units, drain_units, 0)

    def drain_ends(i, _):
        u, owner = i // n_own, lax.rem(i, n_own)

        @pl.when(owner * spread != chip)
        def _():
            end_copy(u, owner).wait_send()

        return 0

    lax.fori_loop(0, units * n_own, drain_ends, 0)

    def drain_carry():
        def one(i, _):
            u, d = i // chips, lax.rem(i, chips)

            @pl.when(d != chip)
            def _():
                carry_copy(u, d).wait_send()

            return 0

        lax.fori_loop(0, units * chips, one, 0)

    if spread == 1:
        drain_carry()
    else:
        pl.when(lax.rem(chip, spread) == 0)(drain_carry)

    def take_sum(d, _):
        @pl.when(d != me_tp)
        def _():
            sum_arrival(d).wait_recv()
            sum_copy(d).wait_send()

        return 0

    lax.fori_loop(0, ntp, take_sum, 0)
    total = sums_in[0]
    for d in range(1, ntp):
        total = total + sums_in[d]
    sums_ref[...] = total


def normalize(gated_hbm, sums_hbm, out_hbm, gv, ov, sums, scale, g_sem, o_sem, s_sem):
    groups = gv.shape[0]

    def part(j):
        return slice(j * WIDE, (j + 1) * WIDE)

    take = pltpu.make_async_copy(sums_hbm, sums, s_sem)
    take.start()
    reads = [
        pltpu.make_async_copy(gated_hbm.at[:, part(j)], gv.at[j], g_sem.at[j])
        for j in range(groups)
    ]
    writes = [
        pltpu.make_async_copy(ov.at[j], out_hbm.at[:, part(j)], o_sem.at[j])
        for j in range(groups)
    ]
    for read in reads:
        read.start()
    take.wait()
    root = jnp.sqrt(sums[0:1, :] / D + 1e-06)
    scale[...] = jnp.broadcast_to(1.0 / root, (LANES, scale.shape[0])).T
    for j in range(groups):
        reads[j].wait()
        for tile in range(SUB):
            lanes = slice(tile * LANES, (tile + 1) * LANES)
            wide = gv[j, :, lanes].astype(jnp.float32) * scale[...]
            ov[j, :, lanes] = wide.astype(jnp.bfloat16)
        writes[j].start()
    for write in writes:
        write.wait()


def per_device(n, ntp, hyena_q, hyena_k, hyena_v, filter_rate, filter_residue, skip):
    rows, width = hyena_q.shape
    groups = width // WIDE
    chips = n // 2
    half = ORDER * groups // 2
    unit = min(ORDER, half)
    units = half // unit
    n_own = min(chips, unit)
    keep = unit // n_own
    tiles = width // LANES
    f32, bf16 = jnp.float32, jnp.bfloat16
    any_space = pl.BlockSpec(memory_space=pl.ANY)
    hbm = pl.BlockSpec(memory_space=pltpu.HBM)
    vmem = pl.BlockSpec(memory_space=pltpu.VMEM)
    dma = pltpu.SemaphoreType.DMA
    gated, sums = pl.pallas_call(
        functools.partial(kernel, n, ntp, n_own),
        out_shape=(
            jax.ShapeDtypeStruct((rows, width), bf16),
            jax.ShapeDtypeStruct((SUB, rows), f32),
        ),
        in_specs=[hbm] * 6,
        out_specs=(any_space, vmem),
        scratch_shapes=[
            pltpu.VMEM((groups, rows, WIDE), bf16),
            pltpu.VMEM((groups, rows, WIDE), bf16),
            pltpu.VMEM((groups, rows, WIDE), bf16),
            pltpu.VMEM((groups, rows, WIDE), bf16),
            pltpu.VMEM((ORDER, width), f32),
            pltpu.VMEM((ORDER, width), f32),
            pltpu.VMEM((tiles, LANES), f32),
            pltpu.VMEM(((tiles + 1) * (ORDER + 1), LANES), f32),
            pltpu.VMEM(((tiles + 1) * (ORDER + 1), LANES), f32),
            pltpu.VMEM((groups, ORDER, SUB, LANES), f32),
            pltpu.VMEM((ORDER, SUB, LANES), f32),
            pltpu.VMEM(((tiles + 1) * (rows + 1), LANES), f32),
            pltpu.VMEM((groups, rows, SUB, LANES), f32),
            pltpu.VMEM((groups, rows // STEP, ORDER, SUB, LANES), f32),
            pltpu.VMEM((2 * half, SUB, LANES), f32),
            pltpu.VMEM((half, SUB, LANES), f32),
            pltpu.VMEM((half, SUB, LANES), f32),
            pltpu.VMEM((units * chips, keep, SUB, LANES), f32),
            pltpu.VMEM((units * chips, keep, SUB, LANES), f32),
            pltpu.VMEM((half, SUB, LANES), f32),
            pltpu.VMEM((half, SUB, LANES), f32),
            pltpu.VMEM((2 * half, SUB, LANES), f32),
            pltpu.VMEM((rows, LANES), f32),
            pltpu.VMEM((SUB, rows), f32),
            pltpu.VMEM((ntp, SUB, rows), f32),
            dma((groups,)),
            dma((groups,)),
            dma((groups,)),
            dma((groups,)),
            dma((3,)),
            dma((units,)),
            dma((units,)),
            dma((units * n_own,)),
            dma((units * chips,)),
            dma((units * chips,)),
            dma((units * n_own,)),
            dma((units,)),
            dma((units,)),
            dma((ntp,)),
            dma((ntp,)),
        ],
        compiler_params=pltpu.CompilerParams(
            collective_id=0,
            has_side_effects=True,
            vmem_limit_bytes=64 * 1024 * 1024 - 131072,
        ),
        cost_estimate=pl.CostEstimate(
            flops=5 * ORDER * rows * width,
            bytes_accessed=8 * rows * width,
            transcendentals=ORDER * width,
        ),
    )(
        hyena_q,
        hyena_k,
        hyena_v,
        filter_rate.T,
        filter_residue.T,
        skip.reshape(tiles, LANES),
    )
    return pl.pallas_call(
        normalize,
        out_shape=jax.ShapeDtypeStruct((rows, width), bf16),
        in_specs=[any_space, any_space],
        out_specs=any_space,
        scratch_shapes=[
            pltpu.VMEM((groups, rows, WIDE), bf16),
            pltpu.VMEM((groups, rows, WIDE), bf16),
            pltpu.VMEM((SUB, rows), f32),
            pltpu.VMEM((rows, LANES), f32),
            dma((groups,)),
            dma((groups,)),
            dma(()),
        ],
        compiler_params=pltpu.CompilerParams(
            vmem_limit_bytes=64 * 1024 * 1024 - 131072
        ),
    )(gated, sums)


def solution(mesh):
    n, ntp = mesh.shape["ctx"], mesh.shape["tp"]
    in_specs = (
        P("ctx", "tp"),
        P("ctx", "tp"),
        P("ctx", "tp"),
        P("tp", None),
        P("tp", None),
        P("tp"),
    )
    return jax.shard_map(
        functools.partial(per_device, n, ntp),
        mesh=mesh,
        in_specs=in_specs,
        out_specs=P("ctx", "tp"),
        check_vma=False,
    )
```
